256 devices in a mesh: wl: 4 (over y), gz: 64 (over x, z, core).
Axes of the slice: x: 4, y: 4, z: 8, core: 2. Of those that a mesh axis runs over, the one named last changes fastest.
Arguments:
- source_fwd: float32 [4, 3, 64, 96, 128], P('wl', None, 'gz'), may hold values from -13 to 13
- source_adj: float32 [4, 3, 64, 96, 128], P('wl', None, 'gz'), may hold values from -13 to 13
- permittivity: float32 [3, 64, 96, 128], P(None, 'gz'), may hold values from 1 to 4
- omegas: float32 [4], P('wl'), may hold values from 0.15 to 0.45
- pml_widths: int32 [3], replicated, may hold values from 2 to 4
- design_mask: int32 [64], P('gz'), may hold values 0 or 1
Outputs:
- gradient: float32 [64, 96, 128], P('gz', 'wl')
The draws below stay inside these ranges and needn't reach their ends.
All inputs are finite; a program needn't handle non-finite values. No bound on the sum of `design_mask` on one device may be relied on, other than what follows from the above.
Results may differ from the reference program's by a relative error of at most 0.0003.
Values sent between devices are 32-bit elements; how exact they have to be, the bound alone decides.
No kernel may reach another device: no remote copies, remote signals or barrier semaphores. Data moves between devices by JAX's collectives and lax.ppermute only.
A program may use at most 64 MiB of HBM per device.

```python
import math
import jax
import jax.numpy as jnp
from jax import lax

NX = 96
NY = 128
ITERS = 3
NZ = 64
NWL = 4


def draw_source_fwd(key, part):
    key = jax.random.fold_in(key, 11)
    first_key = jax.random.fold_in(key, 0)
    return jax.random.normal(first_key, (NWL, 3, NZ, NX, NY), jnp.float32)


def draw_source_adj(key, part):
    key = jax.random.fold_in(key, 23)
    first_key = jax.random.fold_in(key, 0)
    return jax.random.normal(first_key, (NWL, 3, NZ, NX, NY), jnp.float32)


def set_ends(array, own_key, smallest, high):
    shape = array.shape
    place = [jax.random.randint(jax.random.fold_in(own_key, axis), (), 0, shape[axis]) for axis in range(len(shape))]
    array = array.at[tuple(place)].set(smallest)
    longest = shape.index(max(shape))
    place[longest] = (place[longest] + 1) % shape[longest]
    return array.at[tuple(place)].set(high)


def level_of(rng, shape, cuts, smallest, high):
    factor_of, own = 1.0, jax.random.fold_in(rng, 6)
    for dim, parts in cuts:
        draws = jnp.exp(jax.random.uniform(jax.random.fold_in(own, dim), (parts,), jnp.float32, smallest / len(cuts), high / len(cuts)))
        factor_of = factor_of * jnp.repeat(draws, shape[dim] // parts).reshape([-1 if axis == dim else 1 for axis in range(len(shape))])
    return factor_of


def setup_inputs(seed: int = 0) -> dict:
    streams_of = jax.random.split(jax.random.key(seed), 7)
    source_fwd = draw_source_fwd(jax.random.fold_in(streams_of[6], 71), 0)
    source_adj = draw_source_adj(jax.random.fold_in(streams_of[6], 71), 0)
    permittivity = jnp.clip(1.0 + 3.0 * jax.random.uniform(streams_of[2], (3, NZ, NX, NY), jnp.float32) ** level_of(streams_of[2], (3, NZ, NX, NY), ((1, 64),), -0.2, 0.2), 1.0, 4.0)
    omegas = jnp.clip(jnp.exp(math.log(0.45) - 1.0986122 * jax.random.uniform(streams_of[3], (NWL,), jnp.float32) ** level_of(streams_of[3], (NWL,), ((0, 4),), -0.2, 0.2)), 0.15, 0.45)
    pml_widths = jax.random.randint(streams_of[4], (3,), 2, 5).astype(jnp.int32)
    design_mask = set_ends((jax.random.randint(streams_of[5], (NZ,), 0, 2) < 1).astype(jnp.int32), jax.random.fold_in(streams_of[5], 1), 0, 1)
    return {"source_fwd": source_fwd, "source_adj": source_adj, "permittivity": permittivity, "omegas": omegas, "pml_widths": pml_widths, "design_mask": design_mask}


SIGMA_MAX = 1.0


def profile(positions, length, layer_width, angular):
    width_f = layer_width.astype(jnp.float32)
    depth_cells = jnp.clip(jnp.maximum(width_f - positions, positions - (length - 1 - width_f)), 0.0, width_f)
    ratios = SIGMA_MAX * (depth_cells / width_f) ** 3 / angular[:, None]
    denominator = 1.0 + ratios * ratios
    return 1.0 / denominator, -ratios / denominator


def shaped(factor, target):
    return factor[0].reshape(target), factor[1].reshape(target)


def times_factor(factor, component):
    real_part = component[:, :, 0]
    imag_part = component[:, :, 1]
    return jnp.stack([factor[0] * real_part - factor[1] * imag_part, factor[0] * imag_part + factor[1] * real_part], axis=2)


def forward_diff(component, dim_index):
    extent = component.shape[dim_index]
    shifted = jnp.concatenate([lax.slice_in_dim(component, 1, extent, axis=dim_index), jnp.zeros_like(lax.slice_in_dim(component, 0, 1, axis=dim_index))], axis=dim_index)
    return shifted - component


def backward_diff(component, dim_index):
    extent = component.shape[dim_index]
    shifted = jnp.concatenate([jnp.zeros_like(lax.slice_in_dim(component, 0, 1, axis=dim_index)), lax.slice_in_dim(component, 0, extent - 1, axis=dim_index)], axis=dim_index)
    return component - shifted


def operator(fields, angular, permittivity, pml_widths):
    wavecount = fields.shape[0]
    depth_n, rows_x, rows_y = fields.shape[4], fields.shape[5], fields.shape[6]
    pos_x = jnp.arange(rows_x, dtype=jnp.float32)
    pos_y = jnp.arange(rows_y, dtype=jnp.float32)
    pos_z = jnp.arange(depth_n, dtype=jnp.float32)
    x_half = shaped(profile(pos_x + 0.5, rows_x, pml_widths[0], angular), (wavecount, 1, 1, rows_x, 1))
    y_half = shaped(profile(pos_y + 0.5, rows_y, pml_widths[1], angular), (wavecount, 1, 1, 1, rows_y))
    z_half = shaped(profile(pos_z + 0.5, depth_n, pml_widths[2], angular), (wavecount, 1, depth_n, 1, 1))
    x_edge = shaped(profile(pos_x, rows_x, pml_widths[0], angular), (wavecount, 1, 1, rows_x, 1))
    y_edge = shaped(profile(pos_y, rows_y, pml_widths[1], angular), (wavecount, 1, 1, 1, rows_y))
    z_edge = shaped(profile(pos_z, depth_n, pml_widths[2], angular), (wavecount, 1, depth_n, 1, 1))
    elec_x, elec_y, elec_z = fields[:, :, :, 0], fields[:, :, :, 1], fields[:, :, :, 2]
    magn_x = times_factor(y_half, forward_diff(elec_z, 5)) - times_factor(z_half, forward_diff(elec_y, 3))
    magn_y = times_factor(z_half, forward_diff(elec_x, 3)) - times_factor(x_half, forward_diff(elec_z, 4))
    magn_z = times_factor(x_half, forward_diff(elec_y, 4)) - times_factor(y_half, forward_diff(elec_x, 5))
    curl_x = times_factor(y_edge, backward_diff(magn_z, 5)) - times_factor(z_edge, backward_diff(magn_y, 3))
    curl_y = times_factor(z_edge, backward_diff(magn_x, 3)) - times_factor(x_edge, backward_diff(magn_z, 4))
    curl_z = times_factor(x_edge, backward_diff(magn_y, 4)) - times_factor(y_edge, backward_diff(magn_x, 5))
    weight = (angular * angular).reshape(wavecount, 1, 1, 1, 1, 1, 1)
    return jnp.stack([curl_x, curl_y, curl_z], axis=3) - weight * permittivity[None, None, None] * fields


def bilinear(left, right):
    dims = (2, 3, 4, 5)
    left_re, left_im = left[:, :, 0], left[:, :, 1]
    right_re, right_im = right[:, :, 0], right[:, :, 1]
    return jnp.sum(left_re * right_re - left_im * right_im, axis=dims), jnp.sum(left_re * right_im + left_im * right_re, axis=dims)


def complex_div(upper, lower):
    denominator = lower[0] * lower[0] + lower[1] * lower[1]
    return (upper[0] * lower[0] + upper[1] * lower[1]) / denominator, (upper[1] * lower[0] - upper[0] * lower[1]) / denominator


def scale_by(coefficient, fields):
    coef_re = coefficient[0][:, :, None, None, None, None]
    coef_im = coefficient[1][:, :, None, None, None, None]
    fields_re, fields_im = fields[:, :, 0], fields[:, :, 1]
    return jnp.stack([coef_re * fields_re - coef_im * fields_im, coef_re * fields_im + coef_im * fields_re], axis=2)


def cocr(forward_src, adjoint_src, apply_op):
    sources = jnp.stack([forward_src, adjoint_src], axis=1)
    residual = jnp.stack([sources, jnp.zeros_like(sources)], axis=2)
    image = apply_op(residual)
    direction = residual
    pushed = image
    rho_now = bilinear(residual, image)
    gram = bilinear(pushed, pushed)
    solution = jnp.zeros_like(residual)
    for iteration in range(ITERS):
        step_size = complex_div(rho_now, gram)
        solution = solution + scale_by(step_size, direction)
        residual = residual - scale_by(step_size, pushed)
        if iteration + 1 < ITERS:
            image = apply_op(residual)
            rho_next = bilinear(residual, image)
            mix_ratio = complex_div(rho_next, rho_now)
            direction = residual + scale_by(mix_ratio, direction)
            pushed = image + scale_by(mix_ratio, pushed)
            gram = bilinear(pushed, pushed)
            rho_now = rho_next
    return solution


def gradient_terms(solution, angular):
    forward_re, forward_im = solution[:, 0, 0], solution[:, 0, 1]
    adjoint_re, adjoint_im = solution[:, 1, 0], solution[:, 1, 1]
    product = jnp.sum(forward_re * adjoint_re - forward_im * adjoint_im, axis=1)
    return (angular * angular)[:, None, None, None] * product


def reference(source_fwd, source_adj, permittivity, omegas, pml_widths, design_mask):
    def one_wave(inputs_wave):
        forward_src, adjoint_src, angular = inputs_wave
        angular = angular[None]

        def apply_op(fields):
            return operator(fields, angular, permittivity, pml_widths)

        solution = cocr(forward_src[None], adjoint_src[None], apply_op)
        return gradient_terms(solution, angular)[0]

    terms = lax.map(one_wave, (source_fwd, source_adj, omegas))
    return jnp.sum(terms, axis=0) * design_mask.astype(jnp.float32)[:, None, None]
```

```python
import jax
import jax.numpy as jnp
from jax import lax
from jax.experimental import pallas as pl
from jax.experimental.pallas import tpu as pltpu
from jax.sharding import PartitionSpec as P

SIGMA_MAX = 1.0
SHIFT = (0.0, 6.0, 12.0)
ROWS = 8
LANES = 128
GRAM = [(0, 0), (0, 1), (1, 1), (0, 2), (1, 2), (2, 2), (0, 3), (1, 3), (2, 3), (3, 3)]
PRODUCTS = [(i, j) for i in range(3) for j in range(3)]
VM = pltpu.VMEM


def cmul(a, b):
    return a[0] * b[0] - a[1] * b[1], a[0] * b[1] + a[1] * b[0]


def cadd(a, b):
    return a[0] + b[0], a[1] + b[1]


def csub(a, b):
    return a[0] - b[0], a[1] - b[1]


def cdiv(upper, lower):
    den = lower[0] * lower[0] + lower[1] * lower[1]
    return (
        (upper[0] * lower[0] + upper[1] * lower[1]) / den,
        (upper[1] * lower[0] - upper[0] * lower[1]) / den,
    )


def rowids():
    return lax.broadcasted_iota(jnp.int32, (ROWS, LANES), 0)


def laneids():
    return lax.broadcasted_iota(jnp.int32, (ROWS, LANES), 1)


class Shifts:
    def __init__(self):
        self.first_row = rowids() == 0
        self.last_row = rowids() == ROWS - 1
        self.first_lane = laneids() == 0
        self.last_lane = laneids() == LANES - 1

    def x_next(self, cur, nxt):
        return pltpu.roll(jnp.where(self.first_row, nxt, cur), ROWS - 1, 0)

    def x_prev(self, cur, prv):
        return pltpu.roll(jnp.where(self.last_row, prv, cur), 1, 0)

    def y_next(self, cur):
        return jnp.where(self.last_lane, 0.0, pltpu.roll(cur, LANES - 1, 1))

    def y_prev(self, cur):
        return jnp.where(self.first_lane, 0.0, pltpu.roll(cur, 1, 1))


def profile(positions, length, width, angular):
    depth = jnp.clip(jnp.maximum(width - positions, positions - (length - 1 - width)), 0.0, width)
    part = depth / width
    ratios = SIGMA_MAX * (part * part * part) / angular
    denominator = 1.0 + ratios * ratios
    return 1.0 / denominator, -ratios / denominator


def factor_kernel(total_planes, rows_x, widths, omegas, mask, place, fx, fv):
    angular = omegas[0]
    wx = widths[0].astype(jnp.float32)
    wy = widths[1].astype(jnp.float32)
    wz = widths[2].astype(jnp.float32)
    slab = place[0]
    for s in range(rows_x // ROWS):
        pos = (rowids() + s * ROWS).astype(jnp.float32)
        at = pl.ds(s * ROWS, ROWS)
        fx[0, at, :], fx[1, at, :] = profile(pos + 0.5, rows_x, wx, angular)
        fx[2, at, :], fx[3, at, :] = profile(pos, rows_x, wx, angular)
    pos = laneids().astype(jnp.float32)
    fv[0], fv[1] = profile(pos + 0.5, LANES, wy, angular)
    fv[2], fv[3] = profile(pos, LANES, wy, angular)
    plane = jnp.broadcast_to(slab.astype(jnp.float32), (ROWS, LANES))
    fv[4], fv[5] = profile(plane + 0.5, total_planes, wz, angular)
    fv[6], fv[7] = profile(plane, total_planes, wz, angular)
    below_re, below_im = profile(plane - 0.5, total_planes, wz, angular)
    inside = plane > 0.0
    fv[8] = jnp.where(inside, below_re, 0.0)
    fv[9] = jnp.where(inside, below_im, 0.0)
    fv[10] = jnp.broadcast_to(angular * angular, (ROWS, LANES))
    fv[11] = jnp.broadcast_to((slab % 2).astype(jnp.float32), (ROWS, LANES))
    fv[12] = jnp.broadcast_to(mask[0].astype(jnp.float32), (ROWS, LANES))


class Factors:
    def __init__(self, fv, fx):
        self.yh = (fv[0], fv[1])
        self.ye = (fv[2], fv[3])
        self.zh = (fv[4], fv[5])
        self.ze = (fv[6], fv[7])
        self.zb = (fv[8], fv[9])
        self.weight = fv[10]
        self.upper_core = fv[11] > 0.5
        self.fx = fx

    def x(self, s):
        at = pl.ds(s * ROWS, ROWS)
        return (self.fx[0, at, :], self.fx[1, at, :]), (self.fx[2, at, :], self.fx[3, at, :])


ZERO = 0.0


def zeros():
    return jnp.zeros((ROWS, LANES), jnp.float32)


def rmul(factor, real):
    return factor[0] * real, factor[1] * real


def curl_of(fac, sh, xe, hx, hy, hz, hx_b, hy_b, before):
    hy_p, hz_p = before
    dby = lambda h: tuple(p - sh.y_prev(p) for p in h)
    dbx = lambda h, q: tuple(p - sh.x_prev(p, r) for p, r in zip(h, q))
    cx = csub(cmul(fac.ye, dby(hz)), cmul(fac.ze, csub(hy, hy_b)))
    cy = csub(cmul(fac.ze, csub(hx, hx_b)), cmul(xe, dbx(hz, hz_p)))
    cz = csub(cmul(xe, dbx(hy, hy_p)), cmul(fac.ye, dby(hx)))
    return cx, cy, cz


def first_apply(fac, sh, b, rc, rz, eps, q, s, strips, before):
    at = pl.ds(s * ROWS, ROWS)
    after = pl.ds((s + 1) * ROWS, ROWS)
    last = s + 1 == strips
    core = fac.upper_core

    def up(c):
        return jnp.where(core, rz[q, c, at, :], rc[q, c, at, :])

    def dn(c, where):
        return jnp.where(core, rc[q, c, where, :], rz[q, c, where, :])

    ex, ey, ez = (b[q, c, at, :] for c in range(3))
    nxt = lambda c: zeros() if last else b[q, c, after, :]
    xh, xe = fac.x(s)
    dx_ez = sh.x_next(ez, nxt(2)) - ez
    dx_ey = sh.x_next(ey, nxt(1)) - ey
    dy_ez = sh.y_next(ez) - ez
    dy_ex = sh.y_next(ex) - ex
    hx = csub(rmul(fac.yh, dy_ez), rmul(fac.zh, up(1) - ey))
    hy = csub(rmul(fac.zh, up(0) - ex), rmul(xh, dx_ez))
    hz = csub(rmul(xh, dx_ey), rmul(fac.yh, dy_ex))
    bx, by, bz = (dn(c, at) for c in range(3))
    dx_bz = sh.x_next(bz, zeros() if last else dn(2, after)) - bz
    dy_bz = sh.y_next(bz) - bz
    hx_b = csub(rmul(fac.yh, dy_bz), rmul(fac.zb, ey - by))
    hy_b = csub(rmul(fac.zb, ex - bx), rmul(xh, dx_bz))
    curls = curl_of(fac, sh, xe, hx, hy, hz, hx_b, hy_b, before)
    out = []
    for c, e in enumerate((ex, ey, ez)):
        out.append((curls[c][0] - fac.weight * eps[c, at, :] * e, curls[c][1]))
    return out, (hy, hz)


def next_apply(fac, sh, exy, ez_ref, rc, rz, eps, q, s, strips, before, shift):
    at = pl.ds(s * ROWS, ROWS)
    after = pl.ds((s + 1) * ROWS, ROWS)
    last = s + 1 == strips
    core = fac.upper_core
    up = lambda c: tuple(jnp.where(core, rz[c, q, p, at, :], rc[c, q, p, at, :]) for p in range(2))
    dn = lambda c: tuple(jnp.where(core, rc[c, q, p, at, :], rz[c, q, p, at, :]) for p in range(2))
    ex = tuple(exy[0, q, p, at, :] for p in range(2))
    ey = tuple(exy[1, q, p, at, :] for p in range(2))
    ez = tuple(ez_ref[q, p, at, :] for p in range(2))
    ey_n = tuple(zeros() if last else exy[1, q, p, after, :] for p in range(2))
    ez_n = tuple(zeros() if last else ez_ref[q, p, after, :] for p in range(2))
    xh, xe = fac.x(s)
    dfx = lambda v, n: tuple(sh.x_next(a, b) - a for a, b in zip(v, n))
    dfy = lambda v: tuple(sh.y_next(a) - a for a in v)
    hx = csub(cmul(fac.yh, dfy(ez)), cmul(fac.zh, csub(up(1), ey)))
    hy = csub(cmul(fac.zh, csub(up(0), ex)), cmul(xh, dfx(ez, ez_n)))
    hz = csub(cmul(xh, dfx(ey, ey_n)), cmul(fac.yh, dfy(ex)))
    hx_b = csub(dn(0), cmul(fac.zb, ey))
    hy_b = cadd(dn(1), cmul(fac.zb, ex))
    curls = curl_of(fac, sh, xe, hx, hy, hz, hx_b, hy_b, before)
    out = []
    for c, e in enumerate((ex, ey, ez)):
        diagonal = fac.weight * eps[c, at, :] + shift
        out.append(tuple(curls[c][p] - diagonal * e[p] for p in range(2)))
    return out, (hy, hz)


def store_field(fac, sh, field, q, s, strips, held, uxy, uz, sc, sz):
    at = pl.ds(s * ROWS, ROWS)
    for c in range(2):
        for p in range(2):
            uxy[c, q, p, at, :] = field[c][p]
    for p in range(2):
        uz[q, p, at, :] = field[2][p]
    if held is not None:
        store_sends(fac, sh, held, field[2], q, s - 1, sc, sz)
    if s + 1 == strips:
        store_sends(fac, sh, field, (zeros(), zeros()), q, s, sc, sz)


def store_sends(fac, sh, field, ez_n, q, s, sc, sz):
    at = pl.ds(s * ROWS, ROWS)
    xh, _ = fac.x(s)
    ex, ey, ez = field
    dx_ez = tuple(sh.x_next(a, b) - a for a, b in zip(ez, ez_n))
    dy_ez = tuple(sh.y_next(a) - a for a in ez)
    part_x = cadd(cmul(fac.yh, dy_ez), cmul(fac.zh, ey))
    part_y = cadd(cmul(fac.zh, ex), cmul(xh, dx_ez))
    part_y = (-part_y[0], -part_y[1])
    for c, (down, above) in enumerate(((ex, part_x), (ey, part_y))):
        for p in range(2):
            sc[c, q, p, at, :] = jnp.where(fac.upper_core, down[p], above[p])
            sz[c, q, p, at, :] = jnp.where(fac.upper_core, above[p], down[p])


def first_kernel(strips, b, rc, rz, eps, fx, fv, uxy, uz, sc, sz):
    fac, sh = Factors(fv, fx), Shifts()
    for q in range(2):
        nil = (zeros(), zeros())
        before, held = (nil, nil), None
        for s in range(strips):
            field, before = first_apply(fac, sh, b, rc, rz, eps, q, s, strips, before)
            store_field(fac, sh, field, q, s, strips, held, uxy, uz, sc, sz)
            held = field


def second_kernel(strips, exy, ez, rc, rz, eps, fx, fv, uxy, uz, sc, sz):
    fac, sh = Factors(fv, fx), Shifts()
    for q in range(2):
        nil = (zeros(), zeros())
        before, held = (nil, nil), None
        for s in range(strips):
            field, before = next_apply(
                fac, sh, exy, ez, rc, rz, eps, q, s, strips, before, SHIFT[1]
            )
            store_field(fac, sh, field, q, s, strips, held, uxy, uz, sc, sz)
            held = field


def strip_of(uxy, uz, q, s):
    at = pl.ds(s * ROWS, ROWS)
    return [tuple(uxy[c, q, p, at, :] for p in range(2)) for c in range(2)] + [
        tuple(uz[q, p, at, :] for p in range(2))
    ]


def source_of(b, q, s):
    at = pl.ds(s * ROWS, ROWS)
    return [(b[q, c, at, :],) for c in range(3)]


def times(a, b):
    if len(a) == 1 and len(b) == 1:
        return (a[0] * b[0],)
    if len(a) == 1:
        return a[0] * b[0], a[0] * b[1]
    if len(b) == 1:
        return a[0] * b[0], a[1] * b[0]
    return cmul(a, b)


def dot_strip(left, right):
    total = None
    for a, b in zip(left, right):
        term = times(a, b)
        total = term if total is None else tuple(x + y for x, y in zip(total, term))
    return total


def gather_sums(sums):
    lane = lax.broadcasted_iota(jnp.int32, (1, LANES), 1)
    row = jnp.zeros((1, LANES), jnp.float32)
    for (g, q, p), block in sums.items():
        folded = jnp.sum(block, axis=0, keepdims=True)
        whole = jnp.sum(folded, axis=1, keepdims=True)
        row = jnp.where(lane == 4 * g + 2 * p + q, whole, row)
    return row


def add_sums(sums, g, q, term):
    for p, block in enumerate(term):
        key = (g, q, p)
        sums[key] = block if key not in sums else sums[key] + block


def sums_kernel(strips, b, uxy, uz, row):
    sums = {}
    for q in range(2):
        for s in range(strips):
            u = [source_of(b, q, s), strip_of(uxy, uz, q, s)]
            for g, (i, j) in enumerate(GRAM):
                if j < 2:
                    add_sums(sums, g, q, dot_strip(u[i], u[j]))
    row[...] = gather_sums(sums)


def products_kernel(strips, before, b, u1xy, u1z, u2xy, u2z, row, products):
    sums = {}
    for s in range(strips):
        at = pl.ds(s * ROWS, ROWS)
        both = []
        for q in range(2):
            u = [source_of(b, q, s), strip_of(u1xy, u1z, q, s), strip_of(u2xy, u2z, q, s)]
            both.append(u)
            for g, (i, j) in enumerate(GRAM):
                if j == 2:
                    add_sums(sums, g, q, dot_strip(u[i], u[j]))
        place = 0
        for i, j in PRODUCTS:
            for part in dot_strip(both[0][i], both[1][j]):
                products[place, at, :] = part
                place += 1
    row[...] = before[...] + gather_sums(sums)


def third_kernel(strips, before, b, u1xy, u1z, u2xy, u2z, rc, rz, eps, fx, fv, row):
    fac, sh = Factors(fv, fx), Shifts()
    sums = {}
    for q in range(2):
        nil = (zeros(), zeros())
        prior = (nil, nil)
        for s in range(strips):
            u3, prior = next_apply(
                fac, sh, u2xy, u2z, rc, rz, eps, q, s, strips, prior, SHIFT[2]
            )
            u = [source_of(b, q, s), strip_of(u1xy, u1z, q, s), strip_of(u2xy, u2z, q, s), u3]
            for g, (i, j) in enumerate(GRAM):
                if j == 3:
                    add_sums(sums, g, q, dot_strip(u[i], u[j]))
    row[...] = jnp.broadcast_to(before[...] + gather_sums(sums), row.shape)


def coefficients(gram):
    def image_of(v):
        out = [None] * 4
        for i, value in enumerate(v):
            if value is None:
                continue
            out[i + 1] = value if out[i + 1] is None else cadd(out[i + 1], value)
            if SHIFT[i] != 0.0:
                moved = (SHIFT[i] * value[0], SHIFT[i] * value[1])
                out[i] = moved if out[i] is None else cadd(out[i], moved)
        return out

    def plus(a, b):
        if a is None:
            return b
        return a if b is None else cadd(a, b)

    def minus(a, b):
        if b is None:
            return a
        return (-b[0], -b[1]) if a is None else csub(a, b)

    def scaled(factor, v):
        return [None if x is None else cmul(factor, x) for x in v]

    def form(left, right):
        total = None
        for i, a in enumerate(left):
            if a is None:
                continue
            inner = None
            for j, b in enumerate(right):
                if b is not None:
                    inner = plus(inner, cmul(b, gram[min(i, j), max(i, j)]))
            total = plus(total, cmul(a, inner))
        return total

    one = jnp.ones_like(gram[0, 0][0])
    residual = [(one, jnp.zeros_like(one)), None, None, None]
    image = [None, (one, jnp.zeros_like(one)), None, None]
    direction, pushed = residual, image
    rho, size = gram[0, 1], gram[1, 1]
    solution = [None] * 4
    for iteration in range(3):
        step = cdiv(rho, size)
        solution = [plus(a, b) for a, b in zip(solution, scaled(step, direction))]
        if iteration == 2:
            break
        residual = [minus(a, b) for a, b in zip(residual, scaled(step, pushed))]
        image = image_of(residual[:3])
        rho_next = form(residual, image)
        ratio = cdiv(rho_next, rho)
        direction = [plus(a, b) for a, b in zip(residual, scaled(ratio, direction))]
        pushed = [plus(a, b) for a, b in zip(image, scaled(ratio, pushed))]
        size = form(pushed, pushed)
        rho = rho_next
    return solution[:3]


def gradient_kernel(strips, rows, products, fv, out):
    total = jnp.sum(rows[...], axis=0, keepdims=True)
    lane, sub = laneids(), rowids()
    spread = jnp.broadcast_to(total, (ROWS, LANES))
    gram = {}
    for g, pair in enumerate(GRAM):
        parts = []
        for p in range(2):
            mine = lane == 4 * g + 2 * p + sub
            picked = jnp.sum(jnp.where(mine, spread, 0.0), axis=1, keepdims=True)
            parts.append(jnp.broadcast_to(picked, (ROWS, LANES)))
        gram[pair] = tuple(parts)
    coefs = coefficients(gram)
    scale = fv[10] * fv[12]
    one_row = lambda v, q: jnp.broadcast_to(v[q : q + 1, :], (ROWS, LANES))
    weights = []
    for i, j in PRODUCTS:
        left = tuple(one_row(x, 0) for x in coefs[i])
        right = tuple(one_row(x, 1) for x in coefs[j])
        both = cmul(left, right)
        weights.append(both[0] * scale)
        if (i, j) != (0, 0):
            weights.append(-both[1] * scale)
    per_share = strips // out.shape[0]
    for s in range(strips):
        at = pl.ds(s * ROWS, ROWS)
        value = None
        for place, weight in enumerate(weights):
            term = weight * products[place, at, :]
            value = term if value is None else value + term
        out[s // per_share, pl.ds((s % per_share) * ROWS, ROWS), :] = value


def call(kernel, outs, *args, smem=0, name=None, flops=0):
    specs = [pl.BlockSpec(memory_space=pltpu.SMEM if i < smem else VM) for i in range(len(args))]
    shapes = [jax.ShapeDtypeStruct(s, jnp.float32) for s in outs]
    outs_spec = [pl.BlockSpec(memory_space=VM) for _ in outs]
    nbytes = sum(4 * a.size for a in args)
    return pl.pallas_call(
        kernel,
        out_shape=shapes,
        in_specs=specs,
        out_specs=outs_spec,
        name=name,
        cost_estimate=pl.CostEstimate(flops=flops, bytes_accessed=nbytes, transcendentals=0),
        compiler_params=pltpu.CompilerParams(vmem_limit_bytes=32 * 1024 * 1024),
    )(*args)


def partial(fn, *args):
    def inner(*refs):
        fn(*args, *refs)

    return inner


def body(source_fwd, source_adj, permittivity, omegas, pml_widths, design_mask):
    slabs = lax.axis_size("gz")
    shares = lax.axis_size("wl")
    rows_x, rows_y = source_fwd.shape[3], source_fwd.shape[4]
    strips = rows_x // ROWS
    core_pairs = [(i, i ^ 1) for i in range(slabs)]
    chip_pairs = []
    for i in range(1, slabs - 1, 2):
        chip_pairs += [(i, i + 1), (i + 1, i)]
    place = lax.axis_index("gz").astype(jnp.int32).reshape(1)
    b = jnp.concatenate([source_fwd, source_adj], axis=0).reshape(2, 3, rows_x, rows_y)
    eps = permittivity.reshape(3, rows_x, rows_y)
    field = (2, 2, 2, rows_x, rows_y)
    plain = (2, 2, rows_x, rows_y)

    def swap(to_chip, to_core):
        from_chip = lax.ppermute(to_chip, "gz", chip_pairs)
        from_core = lax.ppermute(to_core, "gz", core_pairs)
        return from_core, from_chip

    rc, rz = swap(b, b)
    fx, fv = call(
        partial(factor_kernel, slabs, rows_x),
        [(4, rows_x, rows_y), (13, ROWS, LANES)],
        pml_widths,
        omegas,
        design_mask,
        place,
        smem=4,
        name="factors",
    )
    u1xy, u1z, sc, sz = call(
        partial(first_kernel, strips),
        [field, plain, field, field],
        b,
        rc,
        rz,
        eps,
        fx,
        fv,
        name="apply_first",
    )
    rc, rz = swap(sz, sc)
    (row,) = call(partial(sums_kernel, strips), [(1, LANES)], b, u1xy, u1z, name="sums")
    u2xy, u2z, sc, sz = call(
        partial(second_kernel, strips),
        [field, plain, field, field],
        u1xy,
        u1z,
        rc,
        rz,
        eps,
        fx,
        fv,
        name="apply_second",
    )
    rc, rz = swap(sz, sc)
    row, products = call(
        partial(products_kernel, strips),
        [(1, LANES), (2 * len(PRODUCTS) - 1, rows_x, rows_y)],
        row,
        b,
        u1xy,
        u1z,
        u2xy,
        u2z,
        name="products",
    )
    (rows,) = call(
        partial(third_kernel, strips),
        [(slabs, LANES)],
        row,
        b,
        u1xy,
        u1z,
        u2xy,
        u2z,
        rc,
        rz,
        eps,
        fx,
        fv,
        name="apply_third",
    )
    rows = lax.all_to_all(rows, "gz", 0, 0)
    (parts,) = call(
        partial(gradient_kernel, strips),
        [(shares, rows_x // shares, rows_y)],
        rows,
        products,
        fv,
        name="gradient",
    )
    parts = lax.all_to_all(parts, "wl", 0, 0)
    return jnp.sum(parts, axis=0)[None]


def solution(mesh):
    return jax.shard_map(
        body,
        mesh=mesh,
        in_specs=(
            P("wl", None, "gz", None, None),
            P("wl", None, "gz", None, None),
            P(None, "gz", None, None),
            P("wl"),
            P(),
            P("gz"),
        ),
        out_specs=P("gz", "wl", None),
        check_vma=False,
    )
```

```python
import jax
import jax.numpy as jnp
from jax import lax
from jax.experimental import pallas as pl
from jax.experimental.pallas import tpu as pltpu
from jax.sharding import PartitionSpec as P

SIGMA_MAX = 1.0
SHIFT = (0.0, 6.0, 12.0)
ROWS = 8
LANES = 128
GRAM = [(0, 0), (0, 1), (1, 1), (0, 2), (1, 2), (2, 2), (0, 3), (1, 3), (2, 3), (3, 3)]
PRODUCTS = [(i, j) for i in range(3) for j in range(3)]
VM = pltpu.VMEM


def cmul(a, b):
    return a[0] * b[0] - a[1] * b[1], a[0] * b[1] + a[1] * b[0]


def cadd(a, b):
    return a[0] + b[0], a[1] + b[1]


def csub(a, b):
    return a[0] - b[0], a[1] - b[1]


def cdiv(upper, lower):
    den = lower[0] * lower[0] + lower[1] * lower[1]
    return (
        (upper[0] * lower[0] + upper[1] * lower[1]) / den,
        (upper[1] * lower[0] - upper[0] * lower[1]) / den,
    )


def rowids():
    return lax.broadcasted_iota(jnp.int32, (ROWS, LANES), 0)


def laneids():
    return lax.broadcasted_iota(jnp.int32, (ROWS, LANES), 1)


class Shifts:
    def __init__(self):
        self.first_row = rowids() == 0
        self.last_row = rowids() == ROWS - 1
        self.first_lane = laneids() == 0
        self.last_lane = laneids() == LANES - 1

    def x_next(self, cur, nxt):
        return pltpu.roll(jnp.where(self.first_row, nxt, cur), ROWS - 1, 0)

    def x_prev(self, cur, prv):
        return pltpu.roll(jnp.where(self.last_row, prv, cur), 1, 0)

    def y_next(self, cur):
        return jnp.where(self.last_lane, 0.0, pltpu.roll(cur, LANES - 1, 1))

    def y_prev(self, cur):
        return jnp.where(self.first_lane, 0.0, pltpu.roll(cur, 1, 1))


def profile(positions, length, width, angular):
    depth = jnp.clip(jnp.maximum(width - positions, positions - (length - 1 - width)), 0.0, width)
    part = depth / width
    ratios = SIGMA_MAX * (part * part * part) / angular
    denominator = 1.0 + ratios * ratios
    return 1.0 / denominator, -ratios / denominator


def factor_kernel(total_planes, rows_x, widths, omegas, mask, place, fx, fv):
    angular = omegas[0]
    wx = widths[0].astype(jnp.float32)
    wy = widths[1].astype(jnp.float32)
    wz = widths[2].astype(jnp.float32)
    slab = place[0]
    for s in range(rows_x // ROWS):
        pos = (rowids() + s * ROWS).astype(jnp.float32)
        at = pl.ds(s * ROWS, ROWS)
        fx[0, at, :], fx[1, at, :] = profile(pos + 0.5, rows_x, wx, angular)
        fx[2, at, :], fx[3, at, :] = profile(pos, rows_x, wx, angular)
    pos = laneids().astype(jnp.float32)
    fv[0], fv[1] = profile(pos + 0.5, LANES, wy, angular)
    fv[2], fv[3] = profile(pos, LANES, wy, angular)
    fv[4] = jnp.broadcast_to(angular * angular, (ROWS, LANES))
    fv[5] = jnp.broadcast_to((slab % 2).astype(jnp.float32), (ROWS, LANES))
    fv[6] = jnp.broadcast_to(mask[0].astype(jnp.float32), (ROWS, LANES))
    side = 1 - 2 * (slab % 2)
    for n, at_plane in enumerate((slab, slab - side, slab - 2 * side, slab + side)):
        plane = jnp.broadcast_to(at_plane.astype(jnp.float32), (ROWS, LANES))
        low = 7 + 7 * n
        fv[low], fv[low + 1] = profile(plane + 0.5, total_planes, wz, angular)
        fv[low + 2], fv[low + 3] = profile(plane, total_planes, wz, angular)
        below_re, below_im = profile(plane - 0.5, total_planes, wz, angular)
        above_floor = plane > 0.0
        fv[low + 4] = jnp.where(above_floor, below_re, 0.0)
        fv[low + 5] = jnp.where(above_floor, below_im, 0.0)
        inside = (plane >= 0.0) & (plane < total_planes)
        fv[low + 6] = jnp.where(inside, 1.0, 0.0)


OWN, CHIP, BEHIND, CORE = 0, 1, 2, 3
FACTOR_BLOCKS = 35


class Factors:
    def __init__(self, fv, fx, which=OWN):
        low = 7 + 7 * which
        self.yh = (fv[0], fv[1])
        self.ye = (fv[2], fv[3])
        self.weight = fv[4]
        self.upper_core = fv[5] > 0.5
        self.zh = (fv[low], fv[low + 1])
        self.ze = (fv[low + 2], fv[low + 3])
        self.zb = (fv[low + 4], fv[low + 5])
        self.inside = fv[low + 6]
        self.fx = fx

    def x(self, s):
        at = pl.ds(s * ROWS, ROWS)
        return (self.fx[0, at, :], self.fx[1, at, :]), (self.fx[2, at, :], self.fx[3, at, :])


def zeros():
    return jnp.zeros((ROWS, LANES), jnp.float32)


def no_strip():
    nil = (zeros(), zeros())
    return nil, nil


def rmul(factor, real):
    return factor[0] * real, factor[1] * real


def here(s):
    return pl.ds(s * ROWS, ROWS)


def curl_of(fac, sh, xe, hx, hy, hz, hx_b, hy_b, before):
    hy_p, hz_p = before
    dby = lambda h: tuple(p - sh.y_prev(p) for p in h)
    dbx = lambda h, q: tuple(p - sh.x_prev(p, r) for p, r in zip(h, q))
    cx = csub(cmul(fac.ye, dby(hz)), cmul(fac.ze, csub(hy, hy_b)))
    cy = csub(cmul(fac.ze, csub(hx, hx_b)), cmul(xe, dbx(hz, hz_p)))
    cz = csub(cmul(xe, dbx(hy, hy_p)), cmul(fac.ye, dby(hx)))
    return cx, cy, cz


def real_apply(fac, sh, lo, mid, hi, eps, s, strips, before):
    at = here(s)
    after = lambda of, c: zeros() if s + 1 == strips else of(c, here(s + 1))
    ex, ey, ez = (mid(c, at) for c in range(3))
    xh, xe = fac.x(s)
    dx_ez = sh.x_next(ez, after(mid, 2)) - ez
    dx_ey = sh.x_next(ey, after(mid, 1)) - ey
    dy_ez = sh.y_next(ez) - ez
    dy_ex = sh.y_next(ex) - ex
    hx = csub(rmul(fac.yh, dy_ez), rmul(fac.zh, hi(1, at) - ey))
    hy = csub(rmul(fac.zh, hi(0, at) - ex), rmul(xh, dx_ez))
    hz = csub(rmul(xh, dx_ey), rmul(fac.yh, dy_ex))
    bx, by, bz = (lo(c, at) for c in range(3))
    dx_bz = sh.x_next(bz, after(lo, 2)) - bz
    dy_bz = sh.y_next(bz) - bz
    hx_b = csub(rmul(fac.yh, dy_bz), rmul(fac.zb, ey - by))
    hy_b = csub(rmul(fac.zb, ex - bx), rmul(xh, dx_bz))
    curls = curl_of(fac, sh, xe, hx, hy, hz, hx_b, hy_b, before)
    out = []
    for c, e in enumerate((ex, ey, ez)):
        out.append((curls[c][0] - fac.weight * eps(c, at) * e, curls[c][1]))
    return out, (hy, hz)


def complex_apply(fac, sh, mid, up, below, eps, s, strips, before, shift):
    at = here(s)
    nil = (zeros(), zeros())
    after = lambda c: nil if s + 1 == strips else mid(c, here(s + 1))
    ex, ey, ez = (mid(c, at) for c in range(3))
    xh, xe = fac.x(s)
    dfx = lambda v, n: tuple(sh.x_next(a, b) - a for a, b in zip(v, n))
    dfy = lambda v: tuple(sh.y_next(a) - a for a in v)
    hx = csub(cmul(fac.yh, dfy(ez)), cmul(fac.zh, csub(up(1, at), ey)))
    hy = csub(cmul(fac.zh, csub(up(0, at), ex)), cmul(xh, dfx(ez, after(2))))
    hz = csub(cmul(xh, dfx(ey, after(1))), cmul(fac.yh, dfy(ex)))
    hx_b, hy_b = below(ex, ey)
    curls = curl_of(fac, sh, xe, hx, hy, hz, hx_b, hy_b, before)
    out = []
    for c, e in enumerate((ex, ey, ez)):
        diagonal = fac.weight * eps(c, at) + shift
        out.append(tuple(curls[c][p] - diagonal * e[p] for p in range(2)))
    return out, (hy, hz)


def plane_of(ref, q):
    return lambda c, at: ref[3 * q + c, at, :]


def eps_of(ref):
    return lambda c, at: ref[6 + c, at, :]


def either(mask, yes, no):
    return lambda c, at: jnp.where(mask, yes(c, at), no(c, at))


def field_of(uxy, uz, q):
    def read(c, at):
        ref = uz.at[q] if c == 2 else uxy.at[c, q]
        return ref[0, at, :], ref[1, at, :]

    return read


def side_of(ref, q):
    return lambda c, at: (ref[c, q, 0, at, :], ref[c, q, 1, at, :])


def either_pair(mask, yes, no):
    def read(c, at):
        return tuple(jnp.where(mask, a, b) for a, b in zip(yes(c, at), no(c, at)))

    return read


def store_sends(fac, sh, field, ez_n, q, s, sc, sz):
    at = here(s)
    xh, _ = fac.x(s)
    ex, ey, ez = field
    dx_ez = tuple(sh.x_next(a, b) - a for a, b in zip(ez, ez_n))
    dy_ez = tuple(sh.y_next(a) - a for a in ez)
    part_x = cadd(cmul(fac.yh, dy_ez), cmul(fac.zh, ey))
    part_y = cadd(cmul(fac.zh, ex), cmul(xh, dx_ez))
    part_y = (-part_y[0], -part_y[1])
    for c, (down, above) in enumerate(((ex, part_x), (ey, part_y))):
        for p in range(2):
            if sc is not None:
                sc[c, q, p, at, :] = jnp.where(fac.upper_core, down[p], above[p])
            if sz is not None:
                sz[c, q, p, at, :] = jnp.where(fac.upper_core, above[p], down[p])


def store_field(field, q, s, uxy, uz):
    for p in range(2):
        for c in range(2):
            uxy[c, q, p, here(s), :] = field[c][p]
        uz[q, p, here(s), :] = field[2][p]


def with_sends(fac, sh, q, strips, sc, sz, strips_of):
    held = []

    def store(field, s):
        if held:
            store_sends(fac, sh, held.pop(), field[2], q, s - 1, sc, sz)
        held.append(field)

    strips_of(store)
    store_sends(fac, sh, held.pop(), (zeros(), zeros()), q, strips - 1, sc, sz)


def real_strips(fac, sh, lo, mid, hi, eps, strips, store):
    before = no_strip()
    for s in range(strips):
        field, before = real_apply(fac, sh, lo, mid, hi, eps, s, strips, before)
        store(field, s)


def complex_strips(fac, sh, eps, uxy, uz, rc, rz, q, strips, shift, store):
    core = fac.upper_core
    before = no_strip()
    up = either_pair(core, side_of(rz, q), side_of(rc, q))
    dn = either_pair(core, side_of(rc, q), side_of(rz, q))
    for s in range(strips):

        def below(ex, ey):
            at = here(s)
            return csub(dn(0, at), cmul(fac.zb, ey)), cadd(dn(1, at), cmul(fac.zb, ex))

        field, before = complex_apply(
            fac, sh, field_of(uxy, uz, q), up, below, eps, s, strips, before, shift
        )
        store(field, s)


def masked(fac, field):
    return [tuple(v * fac.inside for v in pair) for pair in field]


def own_kernel(strips, x, ca, za, fx, fv, uxy, uz, sz):
    fac, sh = Factors(fv, fx), Shifts()
    core = fac.upper_core
    for q in range(2):
        hi = either(core, plane_of(za, q), plane_of(ca, q))
        lo = either(core, plane_of(ca, q), plane_of(za, q))

        def run(store):
            def both(field, s):
                store_field(field, q, s, uxy, uz)
                store(field, s)

            real_strips(fac, sh, lo, plane_of(x, q), hi, eps_of(x), strips, both)

        with_sends(fac, sh, q, strips, None, sz, run)


def side_kernel(strips, x, za, zb, fx, fv, uxy, uz, rz):
    fac, sh = Factors(fv, fx, CHIP), Shifts()
    core = fac.upper_core
    for q in range(2):
        hi = either(core, plane_of(zb, q), plane_of(x, q))
        lo = either(core, plane_of(x, q), plane_of(zb, q))

        def run(store):
            def both(field, s):
                field = masked(fac, field)
                store_field(field, q, s, uxy, uz)
                store(field, s)

            real_strips(fac, sh, lo, plane_of(za, q), hi, eps_of(za), strips, both)

        with_sends(fac, sh, q, strips, rz, None, run)


def core_kernel(strips, x, ca, cb, fx, fv, rc):
    fac, sh = Factors(fv, fx, CORE), Shifts()
    core = fac.upper_core
    for q in range(2):
        hi = either(core, plane_of(x, q), plane_of(cb, q))
        lo = either(core, plane_of(cb, q), plane_of(x, q))

        def run(store):
            real_strips(fac, sh, lo, plane_of(ca, q), hi, eps_of(ca), strips, store)

        with_sends(fac, sh, q, strips, None, rc, run)


def second_kernel(strips, x, u1xy, u1z, rc, rz, fx, fv, uxy, uz, sc):
    fac, sh = Factors(fv, fx), Shifts()
    for q in range(2):

        def run(store):
            def both(field, s):
                store_field(field, q, s, uxy, uz)
                store(field, s)

            complex_strips(
                fac, sh, eps_of(x), u1xy, u1z, rc, rz, q, strips, SHIFT[1], both
            )

        with_sends(fac, sh, q, strips, sc, None, run)


def behind_kernel(strips, za, zb, zc, sz, side_xy, side_z, fx, fv, rz2, rz1):
    sh = Shifts()
    for q in range(2):
        fac = Factors(fv, fx, BEHIND)
        core = fac.upper_core
        hi = either(core, plane_of(zc, q), plane_of(za, q))
        lo = either(core, plane_of(za, q), plane_of(zc, q))

        def run_first(store):
            masked_store = lambda field, s: store(masked(fac, field), s)
            real_strips(fac, sh, lo, plane_of(zb, q), hi, eps_of(zb), strips, masked_store)

        with_sends(fac, sh, q, strips, rz1, None, run_first)
    for q in range(2):
        fac = Factors(fv, fx, CHIP)

        def run_second(store):
            masked_store = lambda field, s: store(masked(fac, field), s)
            complex_strips(
                fac, sh, eps_of(za), side_xy, side_z, sz, rz1, q, strips, SHIFT[1], masked_store
            )

        with_sends(fac, sh, q, strips, rz2, None, run_second)


def third_kernel(strips, before, x, u1xy, u1z, u2xy, u2z, rc, rz, fx, fv, row):
    fac, sh = Factors(fv, fx), Shifts()
    sums = {}
    for q in range(2):

        def store(u3, s):
            u = [source_of(x, q, s), strip_of(u1xy, u1z, q, s), strip_of(u2xy, u2z, q, s), u3]
            for g, (i, j) in enumerate(GRAM):
                if j == 3:
                    add_sums(sums, g, q, dot_strip(u[i], u[j]))

        complex_strips(fac, sh, eps_of(x), u2xy, u2z, rc, rz, q, strips, SHIFT[2], store)
    row[...] = jnp.broadcast_to(before[...] + gather_sums(sums), row.shape)


def strip_of(uxy, uz, q, s):
    at = pl.ds(s * ROWS, ROWS)
    return [tuple(uxy[c, q, p, at, :] for p in range(2)) for c in range(2)] + [
        tuple(uz[q, p, at, :] for p in range(2))
    ]


def source_of(x, q, s):
    return [(x[3 * q + c, here(s), :],) for c in range(3)]


def times(a, b):
    if len(a) == 1 and len(b) == 1:
        return (a[0] * b[0],)
    if len(a) == 1:
        return a[0] * b[0], a[0] * b[1]
    if len(b) == 1:
        return a[0] * b[0], a[1] * b[0]
    return cmul(a, b)


def dot_strip(left, right):
    total = None
    for a, b in zip(left, right):
        term = times(a, b)
        total = term if total is None else tuple(x + y for x, y in zip(total, term))
    return total


def gather_sums(sums):
    lane = lax.broadcasted_iota(jnp.int32, (1, LANES), 1)
    row = jnp.zeros((1, LANES), jnp.float32)
    for (g, q, p), block in sums.items():
        folded = jnp.sum(block, axis=0, keepdims=True)
        whole = jnp.sum(folded, axis=1, keepdims=True)
        row = jnp.where(lane == 4 * g + 2 * p + q, whole, row)
    return row


def add_sums(sums, g, q, term):
    for p, block in enumerate(term):
        key = (g, q, p)
        sums[key] = block if key not in sums else sums[key] + block


def sums_kernel(strips, b, uxy, uz, row):
    sums = {}
    for q in range(2):
        for s in range(strips):
            u = [source_of(b, q, s), strip_of(uxy, uz, q, s)]
            for g, (i, j) in enumerate(GRAM):
                if j < 2:
                    add_sums(sums, g, q, dot_strip(u[i], u[j]))
    row[...] = gather_sums(sums)


def products_kernel(strips, before, b, u1xy, u1z, u2xy, u2z, row, products):
    sums = {}
    for s in range(strips):
        at = pl.ds(s * ROWS, ROWS)
        both = []
        for q in range(2):
            u = [source_of(b, q, s), strip_of(u1xy, u1z, q, s), strip_of(u2xy, u2z, q, s)]
            both.append(u)
            for g, (i, j) in enumerate(GRAM):
                if j == 2:
                    add_sums(sums, g, q, dot_strip(u[i], u[j]))
        place = 0
        for i, j in PRODUCTS:
            for part in dot_strip(both[0][i], both[1][j]):
                products[place, at, :] = part
                place += 1
    row[...] = before[...] + gather_sums(sums)


def coefficients(gram):
    def image_of(v):
        out = [None] * 4
        for i, value in enumerate(v):
            if value is None:
                continue
            out[i + 1] = value if out[i + 1] is None else cadd(out[i + 1], value)
            if SHIFT[i] != 0.0:
                moved = (SHIFT[i] * value[0], SHIFT[i] * value[1])
                out[i] = moved if out[i] is None else cadd(out[i], moved)
        return out

    def plus(a, b):
        if a is None:
            return b
        return a if b is None else cadd(a, b)

    def minus(a, b):
        if b is None:
            return a
        return (-b[0], -b[1]) if a is None else csub(a, b)

    def scaled(factor, v):
        return [None if x is None else cmul(factor, x) for x in v]

    def form(left, right):
        total = None
        for i, a in enumerate(left):
            if a is None:
                continue
            inner = None
            for j, b in enumerate(right):
                if b is not None:
                    inner = plus(inner, cmul(b, gram[min(i, j), max(i, j)]))
            total = plus(total, cmul(a, inner))
        return total

    one = jnp.ones_like(gram[0, 0][0])
    residual = [(one, jnp.zeros_like(one)), None, None, None]
    image = [None, (one, jnp.zeros_like(one)), None, None]
    direction, pushed = residual, image
    rho, size = gram[0, 1], gram[1, 1]
    solution = [None] * 4
    for iteration in range(3):
        step = cdiv(rho, size)
        solution = [plus(a, b) for a, b in zip(solution, scaled(step, direction))]
        if iteration == 2:
            break
        residual = [minus(a, b) for a, b in zip(residual, scaled(step, pushed))]
        image = image_of(residual[:3])
        rho_next = form(residual, image)
        ratio = cdiv(rho_next, rho)
        direction = [plus(a, b) for a, b in zip(residual, scaled(ratio, direction))]
        pushed = [plus(a, b) for a, b in zip(image, scaled(ratio, pushed))]
        size = form(pushed, pushed)
        rho = rho_next
    return solution[:3]


def gradient_kernel(strips, rows, products, fv, out):
    total = jnp.sum(rows[...], axis=0, keepdims=True)
    lane, sub = laneids(), rowids()
    spread = jnp.broadcast_to(total, (ROWS, LANES))
    gram = {}
    for g, pair in enumerate(GRAM):
        parts = []
        for p in range(2):
            mine = lane == 4 * g + 2 * p + sub
            picked = jnp.sum(jnp.where(mine, spread, 0.0), axis=1, keepdims=True)
            parts.append(jnp.broadcast_to(picked, (ROWS, LANES)))
        gram[pair] = tuple(parts)
    coefs = coefficients(gram)
    scale = fv[4] * fv[6]
    one_row = lambda v, q: jnp.broadcast_to(v[q : q + 1, :], (ROWS, LANES))
    weights = []
    for i, j in PRODUCTS:
        left = tuple(one_row(x, 0) for x in coefs[i])
        right = tuple(one_row(x, 1) for x in coefs[j])
        both = cmul(left, right)
        weights.append(both[0] * scale)
        if (i, j) != (0, 0):
            weights.append(-both[1] * scale)
    per_share = strips // out.shape[0]
    for s in range(strips):
        at = pl.ds(s * ROWS, ROWS)
        value = None
        for place, weight in enumerate(weights):
            term = weight * products[place, at, :]
            value = term if value is None else value + term
        out[s // per_share, pl.ds((s % per_share) * ROWS, ROWS), :] = value


def call(kernel, outs, *args, smem=0, name=None, flops=0, cost=1, scratch=()):
    specs = [pl.BlockSpec(memory_space=pltpu.SMEM if i < smem else VM) for i in range(len(args))]
    shapes = [jax.ShapeDtypeStruct(s, jnp.float32) for s in outs]
    outs_spec = [pl.BlockSpec(memory_space=VM) for _ in outs]
    return pl.pallas_call(
        kernel,
        out_shape=shapes,
        in_specs=specs,
        out_specs=outs_spec,
        scratch_shapes=[VM(s, jnp.float32) for s in scratch],
        name=name,
        cost_estimate=pl.CostEstimate(flops=flops, bytes_accessed=cost, transcendentals=0),
        compiler_params=pltpu.CompilerParams(vmem_limit_bytes=32 * 1024 * 1024),
    )(*args)


def partial(fn, *args):
    def inner(*refs):
        fn(*args, *refs)

    return inner


def body(source_fwd, source_adj, permittivity, omegas, pml_widths, design_mask):
    slabs = lax.axis_size("gz")
    shares = lax.axis_size("wl")
    rows_x, rows_y = source_fwd.shape[3], source_fwd.shape[4]
    strips = rows_x // ROWS
    core_pairs = [(i, i ^ 1) for i in range(slabs)]
    chip_pairs = []
    for i in range(1, slabs - 1, 2):
        chip_pairs += [(i, i + 1), (i + 1, i)]
    behind_pairs = [(i, i + 2) for i in range(0, slabs - 2, 2)]
    behind_pairs += [(i, i - 2) for i in range(3, slabs, 2)]
    place = lax.axis_index("gz").astype(jnp.int32).reshape(1)
    x = jnp.concatenate(
        [a.reshape(3, rows_x, rows_y) for a in (source_fwd, source_adj, permittivity)], axis=0
    )
    field = (2, 2, 2, rows_x, rows_y)
    plain = (2, 2, rows_x, rows_y)

    def behind(value):
        return lax.ppermute(value, "gz", behind_pairs)

    def core_swap(value):
        return lax.ppermute(value, "gz", core_pairs)

    za = lax.ppermute(x, "gz", chip_pairs)
    zb = behind(x)
    ca = core_swap(x)
    cb = core_swap(za[:6])
    zc = behind(za[:6])
    za, zb, ca, cb = lax.optimization_barrier((za, zb, ca, cb))
    fx, fv = call(
        partial(factor_kernel, slabs, rows_x),
        [(4, rows_x, rows_y), (FACTOR_BLOCKS, ROWS, LANES)],
        pml_widths,
        omegas,
        design_mask,
        place,
        smem=4,
        name="factors",
    )
    u1xy, u1z, sz = call(
        partial(own_kernel, strips), [field, plain, field], x, ca, za, fx, fv, name="apply_own"
    )
    (rc,) = call(partial(core_kernel, strips), [field], x, ca, cb, fx, fv, name="apply_core")
    side_xy, side_z, rz = call(
        partial(side_kernel, strips), [field, plain, field], x, za, zb, fx, fv, name="apply_side"
    )
    (row,) = call(partial(sums_kernel, strips), [(1, LANES)], x, u1xy, u1z, name="sums")
    u2xy, u2z, sc = call(
        partial(second_kernel, strips),
        [field, plain, field],
        x,
        u1xy,
        u1z,
        rc,
        rz,
        fx,
        fv,
        name="apply_second",
    )
    rc = core_swap(sc)
    row, products = call(
        partial(products_kernel, strips),
        [(1, LANES), (2 * len(PRODUCTS) - 1, rows_x, rows_y)],
        row,
        x,
        u1xy,
        u1z,
        u2xy,
        u2z,
        name="products",
    )
    (rz,) = call(
        partial(behind_kernel, strips),
        [field],
        za,
        zb,
        zc,
        sz,
        side_xy,
        side_z,
        fx,
        fv,
        name="apply_behind",
        scratch=[field],
        flops=1 << 36,
        cost=1 << 27,
    )
    (rows,) = call(
        partial(third_kernel, strips),
        [(slabs, LANES)],
        row,
        x,
        u1xy,
        u1z,
        u2xy,
        u2z,
        rc,
        rz,
        fx,
        fv,
        name="apply_third",
    )
    rows = lax.all_to_all(rows, "gz", 0, 0)
    (parts,) = call(
        partial(gradient_kernel, strips),
        [(shares, rows_x // shares, rows_y)],
        rows,
        products,
        fv,
        name="gradient",
    )
    parts = lax.all_to_all(parts, "wl", 0, 0)
    return jnp.sum(parts, axis=0)[None]


def solution(mesh):
    return jax.shard_map(
        body,
        mesh=mesh,
        in_specs=(
            P("wl", None, "gz", None, None),
            P("wl", None, "gz", None, None),
            P(None, "gz", None, None),
            P("wl"),
            P(),
            P("gz"),
        ),
        out_specs=P("gz", "wl", None),
        check_vma=False,
    )
```

```python
import jax
import jax.numpy as jnp
from jax import lax
from jax.experimental import pallas as pl
from jax.experimental.pallas import tpu as pltpu
from jax.sharding import PartitionSpec as P

SIGMA_MAX = 1.0
SHIFT = (0.0, 6.0, 12.0)
ROWS = 8
WIDEST = 4
LANES = 128
GRAM = [(0, 0), (0, 1), (1, 1), (0, 2), (1, 2), (2, 2), (0, 3), (1, 3), (2, 3), (3, 3)]
PRODUCTS = [(i, j) for i in range(3) for j in range(3)]
VM = pltpu.VMEM


def cmul(a, b):
    if a is None:
        return b
    return a[0] * b[0] - a[1] * b[1], a[0] * b[1] + a[1] * b[0]


def cadd(a, b):
    return a[0] + b[0], a[1] + b[1]


def csub(a, b):
    return minus(a[0], b[0]), minus(a[1], b[1])


def minus(a, b):
    if isinstance(b, float):
        return a
    return -b if isinstance(a, float) else a - b


def cdiv(upper, lower):
    den = lower[0] * lower[0] + lower[1] * lower[1]
    return (
        (upper[0] * lower[0] + upper[1] * lower[1]) / den,
        (upper[1] * lower[0] - upper[0] * lower[1]) / den,
    )


def rowids():
    return lax.broadcasted_iota(jnp.int32, (ROWS, LANES), 0)


def laneids():
    return lax.broadcasted_iota(jnp.int32, (ROWS, LANES), 1)


class Shifts:
    def __init__(self):
        self.first_row = rowids() == 0
        self.last_row = rowids() == ROWS - 1
        self.first_lane = laneids() == 0
        self.last_lane = laneids() == LANES - 1

    def x_next(self, cur, nxt):
        return pltpu.roll(jnp.where(self.first_row, nxt, cur), ROWS - 1, 0)

    def x_prev(self, cur, prv):
        return pltpu.roll(jnp.where(self.last_row, prv, cur), 1, 0)

    def y_next(self, cur):
        return jnp.where(self.last_lane, 0.0, pltpu.roll(cur, LANES - 1, 1))

    def y_prev(self, cur):
        return jnp.where(self.first_lane, 0.0, pltpu.roll(cur, 1, 1))


def profile(positions, length, width, angular):
    depth = jnp.clip(jnp.maximum(width - positions, positions - (length - 1 - width)), 0.0, width)
    part = depth / width
    ratios = SIGMA_MAX * (part * part * part) / angular
    denominator = 1.0 + ratios * ratios
    return 1.0 / denominator, -ratios / denominator


def factor_kernel(total_planes, rows_x, widths, omegas, mask, place, fx, fv):
    angular = omegas[0]
    wx = widths[0].astype(jnp.float32)
    wy = widths[1].astype(jnp.float32)
    wz = widths[2].astype(jnp.float32)
    slab = lax.rem(place[0], total_planes)
    for s in range(rows_x // ROWS):
        pos = (rowids() + s * ROWS).astype(jnp.float32)
        at = pl.ds(s * ROWS, ROWS)
        fx[0, at, :], fx[1, at, :] = profile(pos + 0.5, rows_x, wx, angular)
        fx[2, at, :], fx[3, at, :] = profile(pos, rows_x, wx, angular)
    pos = laneids().astype(jnp.float32)
    fv[0], fv[1] = profile(pos + 0.5, LANES, wy, angular)
    fv[2], fv[3] = profile(pos, LANES, wy, angular)
    fv[4] = jnp.broadcast_to(angular * angular, (ROWS, LANES))
    fv[5] = jnp.broadcast_to((slab % 2).astype(jnp.float32), (ROWS, LANES))
    fv[6] = jnp.broadcast_to(mask[0].astype(jnp.float32), (ROWS, LANES))
    side = 1 - 2 * (slab % 2)
    for n, at_plane in enumerate((slab, slab - side, slab - 2 * side)):
        plane = jnp.broadcast_to(at_plane.astype(jnp.float32), (ROWS, LANES))
        low = 7 + 7 * n
        fv[low], fv[low + 1] = profile(plane + 0.5, total_planes, wz, angular)
        fv[low + 2], fv[low + 3] = profile(plane, total_planes, wz, angular)
        below_re, below_im = profile(plane - 0.5, total_planes, wz, angular)
        above_floor = plane > 0.0
        fv[low + 4] = jnp.where(above_floor, below_re, 0.0)
        fv[low + 5] = jnp.where(above_floor, below_im, 0.0)
        inside = (plane >= 0.0) & (plane < total_planes)
        fv[low + 6] = jnp.where(inside, 1.0, 0.0)
    for at, low in ((28, 14), (30, 21)):
        way = cmul((fv[low], fv[low + 1]), (fv[low + 2], fv[low + 3]))
        fv[at], fv[at + 1] = way[0] * fv[low + 6], way[1] * fv[low + 6]


OWN, CHIP, BEHIND = 0, 1, 2
FACTOR_BLOCKS = 32


class Factors:
    def __init__(self, fv, fx, which=OWN):
        low = 7 + 7 * which
        self.yh = (fv[0], fv[1])
        self.ye = (fv[2], fv[3])
        self.weight = fv[4]
        self.upper_core = fv[5] > 0.5
        self.zh = (fv[low], fv[low + 1])
        self.ze = (fv[low + 2], fv[low + 3])
        self.zb = (fv[low + 4], fv[low + 5])
        self.inside = fv[low + 6]
        self.fx = fx

    def x(self, s):
        if s * ROWS >= WIDEST and s * ROWS + ROWS - 0.5 <= self.fx.shape[1] - 1 - WIDEST:
            return None, None
        at = pl.ds(s * ROWS, ROWS)
        return (self.fx[0, at, :], self.fx[1, at, :]), (self.fx[2, at, :], self.fx[3, at, :])


def zeros():
    return jnp.zeros((ROWS, LANES), jnp.float32)


def no_strip():
    nil = (zeros(), zeros())
    return nil, nil


def rmul(factor, real):
    if factor is None:
        return real, 0.0
    return factor[0] * real, factor[1] * real


def here(s):
    return pl.ds(s * ROWS, ROWS)


def curl_of(fac, sh, xe, hx, hy, hz, hx_b, hy_b, before):
    hy_p, hz_p = before
    dby = lambda h: tuple(p - sh.y_prev(p) for p in h)
    dbx = lambda h, q: tuple(p - sh.x_prev(p, r) for p, r in zip(h, q))
    cx = csub(cmul(fac.ye, dby(hz)), cmul(fac.ze, csub(hy, hy_b)))
    cy = csub(cmul(fac.ze, csub(hx, hx_b)), cmul(xe, dbx(hz, hz_p)))
    cz = csub(cmul(xe, dbx(hy, hy_p)), cmul(fac.ye, dby(hx)))
    return cx, cy, cz


def real_apply(fac, sh, lo, mid, hi, eps, s, strips, before):
    at = here(s)
    after = lambda of, c: zeros() if s + 1 == strips else of(c, here(s + 1))
    ex, ey, ez = (mid(c, at) for c in range(3))
    xh, xe = fac.x(s)
    dx_ez = sh.x_next(ez, after(mid, 2)) - ez
    dx_ey = sh.x_next(ey, after(mid, 1)) - ey
    dy_ez = sh.y_next(ez) - ez
    dy_ex = sh.y_next(ex) - ex
    hx = csub(rmul(fac.yh, dy_ez), rmul(fac.zh, hi(1, at) - ey))
    hy = csub(rmul(fac.zh, hi(0, at) - ex), rmul(xh, dx_ez))
    hz = csub(rmul(xh, dx_ey), rmul(fac.yh, dy_ex))
    bx, by, bz = (lo(c, at) for c in range(3))
    dx_bz = sh.x_next(bz, after(lo, 2)) - bz
    dy_bz = sh.y_next(bz) - bz
    hx_b = csub(rmul(fac.yh, dy_bz), rmul(fac.zb, ey - by))
    hy_b = csub(rmul(fac.zb, ex - bx), rmul(xh, dx_bz))
    curls = curl_of(fac, sh, xe, hx, hy, hz, hx_b, hy_b, before)
    out = []
    for c, e in enumerate((ex, ey, ez)):
        diagonal = 0.0 if eps is None else fac.weight * eps(c, at) * e
        out.append((curls[c][0] - diagonal, curls[c][1]))
    return out, (hy, hz)


def complex_apply(fac, sh, mid, up, below, eps, s, strips, before, shift):
    at = here(s)
    nil = (zeros(), zeros())
    after = lambda c: nil if s + 1 == strips else mid(c, here(s + 1))
    ex, ey, ez = (mid(c, at) for c in range(3))
    xh, xe = fac.x(s)
    dfx = lambda v, n: tuple(sh.x_next(a, b) - a for a, b in zip(v, n))
    dfy = lambda v: tuple(sh.y_next(a) - a for a in v)
    hx = csub(cmul(fac.yh, dfy(ez)), cmul(fac.zh, csub(up(1, at), ey)))
    hy = csub(cmul(fac.zh, csub(up(0, at), ex)), cmul(xh, dfx(ez, after(2))))
    hz = csub(cmul(xh, dfx(ey, after(1))), cmul(fac.yh, dfy(ex)))
    hx_b, hy_b = below(ex, ey)
    curls = curl_of(fac, sh, xe, hx, hy, hz, hx_b, hy_b, before)
    out = []
    for c, e in enumerate((ex, ey, ez)):
        diagonal = fac.weight * eps(c, at) + shift
        out.append(tuple(curls[c][p] - diagonal * e[p] for p in range(2)))
    return out, (hy, hz)


def plane_of(ref, q):
    return lambda c, at: ref[3 * q + c, at, :]


def eps_of(ref, first=6):
    return lambda c, at: ref[first + c, at, :]


def either(mask, yes, no):
    return lambda c, at: jnp.where(mask, yes(c, at), no(c, at))


def field_of(uxy, uz, q):
    def read(c, at):
        ref = uz.at[q] if c == 2 else uxy.at[c, q]
        return ref[0, at, :], ref[1, at, :]

    return read


def side_of(ref, q):
    return lambda c, at: tuple(part_of(ref, c)[q, p, at, :] for p in range(2))


def either_pair(mask, yes, no):
    def read(c, at):
        return tuple(jnp.where(mask, a, b) for a, b in zip(yes(c, at), no(c, at)))

    return read


def part_of(ref, c):
    return ref[c] if isinstance(ref, tuple) else ref.at[c]


def store_sends(fac, sh, field, ez_n, q, s, sc, sz):
    at = here(s)
    xh, _ = fac.x(s)
    ex, ey, ez = field
    dx_ez = tuple(sh.x_next(a, b) - a for a, b in zip(ez, ez_n))
    dy_ez = tuple(sh.y_next(a) - a for a in ez)
    part_x = cadd(cmul(fac.yh, dy_ez), cmul(fac.zh, ey))
    part_y = cadd(cmul(fac.zh, ex), cmul(xh, dx_ez))
    part_y = (-part_y[0], -part_y[1])
    for c, (down, above) in enumerate(((ex, part_x), (ey, part_y))):
        for p in range(2):
            if sc is not None:
                part_of(sc, c)[q, p, at, :] = jnp.where(fac.upper_core, down[p], above[p])
            if sz is not None:
                sz[c, q, p, at, :] = jnp.where(fac.upper_core, above[p], down[p])


def store_field(field, q, s, uxy, uz):
    for p in range(2):
        for c in range(2):
            uxy[c, q, p, here(s), :] = field[c][p]
        uz[q, p, here(s), :] = field[2][p]


def with_sends(fac, sh, q, strips, sc, sz, strips_of):
    held = []

    def store(field, s):
        if held:
            store_sends(fac, sh, held.pop(), field[2], q, s - 1, sc, sz)
        held.append(field)

    strips_of(store)
    store_sends(fac, sh, held.pop(), (zeros(), zeros()), q, strips - 1, sc, sz)


def real_strips(fac, sh, lo, mid, hi, eps, strips, store):
    before = no_strip()
    for s in range(strips):
        field, before = real_apply(fac, sh, lo, mid, hi, eps, s, strips, before)
        store(field, s)


def complex_strips(fac, sh, eps, uxy, uz, rc, rz, q, strips, shift, store):
    core = fac.upper_core
    before = no_strip()
    up = either_pair(core, side_of(rz, q), side_of(rc, q))
    dn = either_pair(core, side_of(rc, q), side_of(rz, q))
    for s in range(strips):

        def below(ex, ey):
            at = here(s)
            return csub(dn(0, at), cmul(fac.zb, ey)), cadd(dn(1, at), cmul(fac.zb, ex))

        field, before = complex_apply(
            fac, sh, field_of(uxy, uz, q), up, below, eps, s, strips, before, shift
        )
        store(field, s)


def masked(fac, field):
    return [tuple(v * fac.inside for v in pair) for pair in field]


def pack_kernel(sources, eps, out):
    out[0:6] = sources[0:6]
    out[6:9] = eps[6:9]


def own_kernel(strips, x, ca, za, fx, fv, uxy, uz, scx, scy, sz):
    fac, sh = Factors(fv, fx), Shifts()
    core = fac.upper_core
    for q in range(2):
        hi = either(core, plane_of(za, q), plane_of(ca, q))
        lo = either(core, plane_of(ca, q), plane_of(za, q))

        def run(store):
            def both(field, s):
                store_field(field, q, s, uxy, uz)
                store(field, s)

            real_strips(fac, sh, lo, plane_of(x, q), hi, eps_of(x), strips, both)

        with_sends(fac, sh, q, strips, (scx, scy), sz, run)


def side_kernel(strips, x, za, zb, fx, fv, uxy, uz, rz):
    fac, sh = Factors(fv, fx, CHIP), Shifts()
    core = fac.upper_core
    for q in range(2):
        hi = either(core, plane_of(zb, q), plane_of(x, q))
        lo = either(core, plane_of(x, q), plane_of(zb, q))

        def run(store):
            def both(field, s):
                field = masked(fac, field)
                store_field(field, q, s, uxy, uz)
                store(field, s)

            real_strips(fac, sh, lo, plane_of(za, q), hi, eps_of(zb), strips, both)

        with_sends(fac, sh, q, strips, rz, None, run)


def second_kernel(strips, x, u1xy, u1z, rcx, rcy, rz, fx, fv, uxy, uz, sc):
    fac, sh = Factors(fv, fx), Shifts()
    for q in range(2):

        def run(store):
            def both(field, s):
                store_field(field, q, s, uxy, uz)
                store(field, s)

            complex_strips(
                fac, sh, eps_of(x), u1xy, u1z, (rcx, rcy), rz, q, strips, SHIFT[1], both
            )

        with_sends(fac, sh, q, strips, sc, None, run)


def behind_kernel(strips, za, zb, fx, fv, rz):
    fac, sh = Factors(fv, fx, BEHIND), Shifts()
    core = fac.upper_core
    for q in range(2):
        near = plane_of(za, q)
        hi = lambda c, at: jnp.where(core, 0.0, near(c, at))
        lo = lambda c, at: jnp.where(core, near(c, at), 0.0)

        def run(store):
            masked_store = lambda field, s: store(masked(fac, field), s)
            real_strips(fac, sh, lo, plane_of(zb, q), hi, None, strips, masked_store)

        with_sends(fac, sh, q, strips, rz, None, run)


def side_second_kernel(strips, zb, rz, sz, side_xy, side_z, fx, fv, out):
    fac, sh = Factors(fv, fx, CHIP), Shifts()
    for q in range(2):

        def run(store):
            masked_store = lambda field, s: store(masked(fac, field), s)
            complex_strips(
                fac, sh, eps_of(zb), side_xy, side_z, sz, rz, q, strips, SHIFT[1], masked_store
            )

        with_sends(fac, sh, q, strips, out, None, run)


def halo_form(fac, sh, zh, s, fields, ez_n):
    ex, ey, ez = fields
    xh, _ = fac.x(s)
    part_x = cadd(rmul(fac.yh, sh.y_next(ez) - ez), rmul(zh, ey))
    part_y = csub(rmul(zh, -ex), rmul(xh, sh.x_next(ez, ez_n) - ez))
    return [
        (jnp.where(fac.upper_core, down, above[0]), jnp.where(fac.upper_core, 0.0, above[1]))
        for down, above in ((ex, part_x), (ey, part_y))
    ]


def far_kernel(strips, rz, zb, zc, fx, fv, out):
    fac, sh = Factors(fv, fx, BEHIND), Shifts()
    near_way, far_way = (fv[28], fv[29]), (fv[30], fv[31])
    for q in range(2):

        def scaled(c, at):
            return zc[6 + c, at, :] * zb[3 * q + c, at, :]

        def far(c, at):
            return zc[3 * q + c, at, :]

        for s in range(strips):
            at = here(s)
            forms = []
            for read, zh in ((scaled, fac.zh), (far, fac.zb)):
                ez_n = zeros() if s + 1 == strips else read(2, here(s + 1))
                forms.append(halo_form(fac, sh, zh, s, [read(c, at) for c in range(3)], ez_n))
            for c in range(2):
                diagonal = (fac.weight * forms[0][c][0], fac.weight * forms[0][c][1])
                change = cmul(near_way, cadd(diagonal, cmul(far_way, forms[1][c])))
                for p in range(2):
                    out[c, q, p, at, :] = rz[c, q, p, at, :] + change[p]


def third_kernel(strips, before, x, u1xy, u1z, u2xy, u2z, rc, rz, fx, fv, row):
    fac, sh = Factors(fv, fx), Shifts()
    sums = {}
    for q in range(2):

        def store(u3, s):
            u = [source_of(x, q, s), strip_of(u1xy, u1z, q, s), strip_of(u2xy, u2z, q, s), u3]
            for g, (i, j) in enumerate(GRAM):
                if j == 3:
                    add_sums(sums, g, q, dot_strip(u[i], u[j]))

        complex_strips(fac, sh, eps_of(x), u2xy, u2z, rc, rz, q, strips, SHIFT[2], store)
    row[...] = jnp.broadcast_to(before[...] + gather_sums(sums), row.shape)


def strip_of(uxy, uz, q, s):
    at = pl.ds(s * ROWS, ROWS)
    return [tuple(uxy[c, q, p, at, :] for p in range(2)) for c in range(2)] + [
        tuple(uz[q, p, at, :] for p in range(2))
    ]


def source_of(x, q, s):
    return [(x[3 * q + c, here(s), :],) for c in range(3)]


def times(a, b):
    if len(a) == 1 and len(b) == 1:
        return (a[0] * b[0],)
    if len(a) == 1:
        return a[0] * b[0], a[0] * b[1]
    if len(b) == 1:
        return a[0] * b[0], a[1] * b[0]
    return cmul(a, b)


def dot_strip(left, right):
    total = None
    for a, b in zip(left, right):
        term = times(a, b)
        total = term if total is None else tuple(x + y for x, y in zip(total, term))
    return total


def gather_sums(sums):
    lane = lax.broadcasted_iota(jnp.int32, (1, LANES), 1)
    row = jnp.zeros((1, LANES), jnp.float32)
    for (g, q, p), block in sums.items():
        folded = jnp.sum(block, axis=0, keepdims=True)
        whole = jnp.sum(folded, axis=1, keepdims=True)
        row = jnp.where(lane == 4 * g + 2 * p + q, whole, row)
    return row


def add_sums(sums, g, q, term):
    for p, block in enumerate(term):
        key = (g, q, p)
        sums[key] = block if key not in sums else sums[key] + block


def sums_kernel(strips, b, uxy, uz, row):
    sums = {}
    for q in range(2):
        for s in range(strips):
            u = [source_of(b, q, s), strip_of(uxy, uz, q, s)]
            for g, (i, j) in enumerate(GRAM):
                if j < 2:
                    add_sums(sums, g, q, dot_strip(u[i], u[j]))
    row[...] = gather_sums(sums)


def products_kernel(strips, before, b, u1xy, u1z, u2xy, u2z, row, products):
    sums = {}
    for s in range(strips):
        at = pl.ds(s * ROWS, ROWS)
        both = []
        for q in range(2):
            u = [source_of(b, q, s), strip_of(u1xy, u1z, q, s), strip_of(u2xy, u2z, q, s)]
            both.append(u)
            for g, (i, j) in enumerate(GRAM):
                if j == 2:
                    add_sums(sums, g, q, dot_strip(u[i], u[j]))
        place = 0
        for i, j in PRODUCTS:
            for part in dot_strip(both[0][i], both[1][j]):
                products[place, at, :] = part
                place += 1
    row[...] = before[...] + gather_sums(sums)


def coefficients(gram):
    def image_of(v):
        out = [None] * 4
        for i, value in enumerate(v):
            if value is None:
                continue
            out[i + 1] = value if out[i + 1] is None else cadd(out[i + 1], value)
            if SHIFT[i] != 0.0:
                moved = (SHIFT[i] * value[0], SHIFT[i] * value[1])
                out[i] = moved if out[i] is None else cadd(out[i], moved)
        return out

    def plus(a, b):
        if a is None:
            return b
        return a if b is None else cadd(a, b)

    def less(a, b):
        if b is None:
            return a
        return (-b[0], -b[1]) if a is None else csub(a, b)

    def scaled(factor, v):
        return [None if x is None else cmul(factor, x) for x in v]

    def form(left, right):
        total = None
        for i, a in enumerate(left):
            if a is None:
                continue
            inner = None
            for j, b in enumerate(right):
                if b is not None:
                    inner = plus(inner, cmul(b, gram[min(i, j), max(i, j)]))
            total = plus(total, cmul(a, inner))
        return total

    one = jnp.ones_like(gram[0, 0][0])
    residual = [(one, jnp.zeros_like(one)), None, None, None]
    image = [None, (one, jnp.zeros_like(one)), None, None]
    direction, pushed = residual, image
    rho, size = gram[0, 1], gram[1, 1]
    solution = [None] * 4
    for iteration in range(3):
        step = cdiv(rho, size)
        solution = [plus(a, b) for a, b in zip(solution, scaled(step, direction))]
        if iteration == 2:
            break
        residual = [less(a, b) for a, b in zip(residual, scaled(step, pushed))]
        image = image_of(residual[:3])
        rho_next = form(residual, image)
        ratio = cdiv(rho_next, rho)
        direction = [plus(a, b) for a, b in zip(residual, scaled(ratio, direction))]
        pushed = [plus(a, b) for a, b in zip(image, scaled(ratio, pushed))]
        size = form(pushed, pushed)
        rho = rho_next
    return solution[:3]


def gradient_kernel(strips, slabs, place, rows, products, fv, *outs):
    total = jnp.sum(rows[...], axis=0, keepdims=True)
    lane, sub = laneids(), rowids()
    spread = jnp.broadcast_to(total, (ROWS, LANES))
    gram = {}
    for g, pair in enumerate(GRAM):
        parts = []
        for p in range(2):
            mine = lane == 4 * g + 2 * p + sub
            picked = jnp.sum(jnp.where(mine, spread, 0.0), axis=1, keepdims=True)
            parts.append(jnp.broadcast_to(picked, (ROWS, LANES)))
        gram[pair] = tuple(parts)
    coefs = coefficients(gram)
    scale = fv[4] * fv[6]
    one_row = lambda v, q: jnp.broadcast_to(v[q : q + 1, :], (ROWS, LANES))
    weights = []
    for i, j in PRODUCTS:
        left = tuple(one_row(x, 0) for x in coefs[i])
        right = tuple(one_row(x, 1) for x in coefs[j])
        both = cmul(left, right)
        weights.append(both[0] * scale)
        if (i, j) != (0, 0):
            weights.append(-both[1] * scale)
    mine, shares = lax.div(place[0], slabs), len(outs)
    for k, out in enumerate(outs):
        theirs = lax.rem(mine + k, shares) * (strips // shares)
        for s in range(strips // shares):
            at = pl.ds(pl.multiple_of((theirs + s) * ROWS, ROWS), ROWS)
            value = None
            for n, weight in enumerate(weights):
                term = weight * products[n, at, :]
                value = term if value is None else value + term
            out[here(s), :] = value


def call(kernel, outs, *args, smem=0, name=None, flops=0, cost=1, scratch=()):
    specs = [pl.BlockSpec(memory_space=pltpu.SMEM if i < smem else VM) for i in range(len(args))]
    shapes = [jax.ShapeDtypeStruct(s, jnp.float32) for s in outs]
    outs_spec = [pl.BlockSpec(memory_space=VM) for _ in outs]
    return pl.pallas_call(
        kernel,
        out_shape=shapes,
        in_specs=specs,
        out_specs=outs_spec,
        scratch_shapes=[VM(s, jnp.float32) for s in scratch],
        name=name,
        cost_estimate=pl.CostEstimate(flops=flops, bytes_accessed=cost, transcendentals=0),
        compiler_params=pltpu.CompilerParams(vmem_limit_bytes=12 * 1024 * 1024),
    )(*args)


def partial(fn, *args):
    def inner(*refs):
        fn(*args, *refs)

    return inner


def body(source_fwd, source_adj, permittivity, omegas, pml_widths, design_mask):
    slabs = lax.axis_size("gz")
    shares = lax.axis_size("wl")
    rows_x, rows_y = source_fwd.shape[3], source_fwd.shape[4]
    strips = rows_x // ROWS
    core_pairs = [(i, i ^ 1) for i in range(slabs)]
    chip_pairs = []
    for i in range(1, slabs - 1, 2):
        chip_pairs += [(i, i + 1), (i + 1, i)]
    behind_pairs = [(i, i + 2) for i in range(0, slabs - 2, 2)]
    behind_pairs += [(i, i - 2) for i in range(3, slabs, 2)]
    place = lax.axis_index(("wl", "gz")).astype(jnp.int32).reshape(1)
    x = jnp.concatenate(
        [a.reshape(3, rows_x, rows_y) for a in (source_fwd, source_adj, permittivity)], axis=0
    )
    field = (2, 2, 2, rows_x, rows_y)
    plain = (2, 2, rows_x, rows_y)

    def behind(value):
        return lax.ppermute(value, "gz", behind_pairs)

    def core_swap(value):
        return lax.ppermute(value, "gz", core_pairs)

    x = lax.optimization_barrier(x)
    ca = core_swap(x)
    za = lax.ppermute(x[:6], "gz", chip_pairs)
    fx, fv = call(
        partial(factor_kernel, slabs, rows_x),
        [(4, rows_x, rows_y), (FACTOR_BLOCKS, ROWS, LANES)],
        pml_widths,
        omegas,
        design_mask,
        place,
        smem=4,
        name="factors",
    )
    ca, fx, fv = lax.optimization_barrier((ca, fx, fv))
    (pack,) = call(pack_kernel, [(9, rows_x, rows_y)], x, ca, name="pack")
    zb = behind(pack)
    (relay,) = call(pack_kernel, [(9, rows_x, rows_y)], za, x, name="pack_relay")
    zc = behind(relay)
    u1xy, u1z, scx, scy, sz = call(
        partial(own_kernel, strips),
        [field, plain, plain, plain, field],
        x,
        ca,
        za,
        fx,
        fv,
        name="apply_own",
    )
    rcx, rcy = core_swap(scx), core_swap(scy)
    side_xy, side_z, rz = call(
        partial(side_kernel, strips), [field, plain, field], x, za, zb, fx, fv, name="apply_side"
    )
    (row,) = call(partial(sums_kernel, strips), [(1, LANES)], x, u1xy, u1z, name="sums")
    u2xy, u2z, sc = call(
        partial(second_kernel, strips),
        [field, plain, field],
        x,
        u1xy,
        u1z,
        rcx,
        rcy,
        rz,
        fx,
        fv,
        name="apply_second",
    )
    rc = core_swap(sc)
    row, products = call(
        partial(products_kernel, strips),
        [(1, LANES), (2 * len(PRODUCTS) - 1, rows_x, rows_y)],
        row,
        x,
        u1xy,
        u1z,
        u2xy,
        u2z,
        name="products",
    )
    sz, row, products = lax.optimization_barrier((sz, row, products))
    (rz,) = call(partial(behind_kernel, strips), [field], za, zb, fx, fv, name="apply_behind")
    (rz,) = call(
        partial(side_second_kernel, strips),
        [field],
        zb,
        rz,
        sz,
        side_xy,
        side_z,
        fx,
        fv,
        name="apply_side_second",
    )
    (rz,) = call(
        partial(far_kernel, strips),
        [field],
        rz,
        zb,
        zc,
        fx,
        fv,
        name="add_far",
        flops=1 << 36,
        cost=1 << 27,
    )
    (rows,) = call(
        partial(third_kernel, strips),
        [(slabs, LANES)],
        row,
        x,
        u1xy,
        u1z,
        u2xy,
        u2z,
        rc,
        rz,
        fx,
        fv,
        name="apply_third",
    )
    rows = lax.all_to_all(rows, "gz", 0, 0)
    parts = call(
        partial(gradient_kernel, strips, slabs),
        [(rows_x // shares, rows_y)] * shares,
        place,
        rows,
        products,
        fv,
        smem=1,
        name="gradient",
    )
    total = parts[0]
    for k in range(1, shares):
        total = total + lax.ppermute(parts[k], "wl", [(i, (i + k) % shares) for i in range(shares)])
    return total[None]


def solution(mesh):
    return jax.shard_map(
        body,
        mesh=mesh,
        in_specs=(
            P("wl", None, "gz", None, None),
            P("wl", None, "gz", None, None),
            P(None, "gz", None, None),
            P("wl"),
            P(),
            P("gz"),
        ),
        out_specs=P("gz", "wl", None),
        check_vma=False,
    )
```

```python
import jax
import jax.numpy as jnp
from jax import lax
from jax.experimental import pallas as pl
from jax.experimental.pallas import tpu as pltpu
from jax.sharding import PartitionSpec as P

SIGMA_MAX = 1.0
SHIFT = (0.0, 6.0, 12.0)
ROWS = 8
WIDEST = 4
LANES = 128
GRAM = [(0, 0), (0, 1), (1, 1), (0, 2), (1, 2), (2, 2), (0, 3), (1, 3), (2, 3), (3, 3)]
PRODUCTS = [(i, j) for i in range(3) for j in range(3)]
VM = pltpu.VMEM


def cmul(a, b):
    if a is None:
        return b
    return a[0] * b[0] - a[1] * b[1], a[0] * b[1] + a[1] * b[0]


def cadd(a, b):
    return a[0] + b[0], a[1] + b[1]


def csub(a, b):
    return minus(a[0], b[0]), minus(a[1], b[1])


def minus(a, b):
    if isinstance(b, float):
        return a
    return -b if isinstance(a, float) else a - b


def cdiv(upper, lower):
    den = lower[0] * lower[0] + lower[1] * lower[1]
    return (
        (upper[0] * lower[0] + upper[1] * lower[1]) / den,
        (upper[1] * lower[0] - upper[0] * lower[1]) / den,
    )


def rowids():
    return lax.broadcasted_iota(jnp.int32, (ROWS, LANES), 0)


def laneids():
    return lax.broadcasted_iota(jnp.int32, (ROWS, LANES), 1)


class Shifts:
    def __init__(self):
        self.first_row = rowids() == 0
        self.last_row = rowids() == ROWS - 1
        self.first_lane = laneids() == 0
        self.last_lane = laneids() == LANES - 1

    def x_next(self, cur, nxt):
        return pltpu.roll(jnp.where(self.first_row, nxt, cur), ROWS - 1, 0)

    def x_prev(self, cur, prv):
        return pltpu.roll(jnp.where(self.last_row, prv, cur), 1, 0)

    def y_next(self, cur):
        return jnp.where(self.last_lane, 0.0, pltpu.roll(cur, LANES - 1, 1))

    def y_prev(self, cur):
        return jnp.where(self.first_lane, 0.0, pltpu.roll(cur, 1, 1))


def profile(positions, length, width, angular):
    depth = jnp.clip(jnp.maximum(width - positions, positions - (length - 1 - width)), 0.0, width)
    part = depth / width
    ratios = SIGMA_MAX * (part * part * part) / angular
    denominator = 1.0 + ratios * ratios
    return 1.0 / denominator, -ratios / denominator


def factor_kernel(total_planes, rows_x, small, fx, fv):
    angular, wx, wy, wz, mask, slab, upper = (
        jnp.broadcast_to(small[:, n : n + 1], (ROWS, LANES)) for n in range(7)
    )
    for s in range(rows_x // ROWS):
        pos = (rowids() + s * ROWS).astype(jnp.float32)
        at = pl.ds(s * ROWS, ROWS)
        fx[0, at, :], fx[1, at, :] = profile(pos + 0.5, rows_x, wx, angular)
        fx[2, at, :], fx[3, at, :] = profile(pos, rows_x, wx, angular)
    pos = laneids().astype(jnp.float32)
    fv[0], fv[1] = profile(pos + 0.5, LANES, wy, angular)
    fv[2], fv[3] = profile(pos, LANES, wy, angular)
    fv[4] = angular * angular
    fv[5] = upper
    fv[6] = mask
    side = 1.0 - 2.0 * upper
    for n, plane in enumerate((slab, slab - side, slab - 2.0 * side)):
        low = 7 + 7 * n
        fv[low], fv[low + 1] = profile(plane + 0.5, total_planes, wz, angular)
        fv[low + 2], fv[low + 3] = profile(plane, total_planes, wz, angular)
        below_re, below_im = profile(plane - 0.5, total_planes, wz, angular)
        above_floor = plane > 0.0
        fv[low + 4] = jnp.where(above_floor, below_re, 0.0)
        fv[low + 5] = jnp.where(above_floor, below_im, 0.0)
        inside = (plane >= 0.0) & (plane < total_planes)
        fv[low + 6] = jnp.where(inside, 1.0, 0.0)
    for at, low in ((28, 14), (30, 21)):
        way = cmul((fv[low], fv[low + 1]), (fv[low + 2], fv[low + 3]))
        fv[at], fv[at + 1] = way[0] * fv[low + 6], way[1] * fv[low + 6]


OWN, CHIP, BEHIND = 0, 1, 2
FACTOR_BLOCKS = 32


class Factors:
    def __init__(self, fv, fx, which=OWN):
        low = 7 + 7 * which
        self.yh = (fv[0], fv[1])
        self.ye = (fv[2], fv[3])
        self.weight = fv[4]
        self.upper_core = fv[5] > 0.5
        self.zh = (fv[low], fv[low + 1])
        self.ze = (fv[low + 2], fv[low + 3])
        self.zb = (fv[low + 4], fv[low + 5])
        self.inside = fv[low + 6]
        self.fx = fx

    def x(self, s):
        if s * ROWS >= WIDEST and s * ROWS + ROWS - 0.5 <= self.fx.shape[1] - 1 - WIDEST:
            return None, None
        at = pl.ds(s * ROWS, ROWS)
        return (self.fx[0, at, :], self.fx[1, at, :]), (self.fx[2, at, :], self.fx[3, at, :])


def zeros():
    return jnp.zeros((ROWS, LANES), jnp.float32)


def no_strip():
    nil = (zeros(), zeros())
    return nil, nil


def rmul(factor, real):
    if factor is None:
        return real, 0.0
    return factor[0] * real, factor[1] * real


def here(s):
    return pl.ds(s * ROWS, ROWS)


def curl_of(fac, sh, xe, hx, hy, hz, hx_b, hy_b, before):
    hy_p, hz_p = before
    dby = lambda h: tuple(p - sh.y_prev(p) for p in h)
    dbx = lambda h, q: tuple(p - sh.x_prev(p, r) for p, r in zip(h, q))
    cx = csub(cmul(fac.ye, dby(hz)), cmul(fac.ze, csub(hy, hy_b)))
    cy = csub(cmul(fac.ze, csub(hx, hx_b)), cmul(xe, dbx(hz, hz_p)))
    cz = csub(cmul(xe, dbx(hy, hy_p)), cmul(fac.ye, dby(hx)))
    return cx, cy, cz


def real_apply(fac, sh, lo, mid, hi, eps, s, strips, before):
    at = here(s)
    after = lambda of, c: zeros() if s + 1 == strips else of(c, here(s + 1))
    ex, ey, ez = (mid(c, at) for c in range(3))
    xh, xe = fac.x(s)
    dx_ez = sh.x_next(ez, after(mid, 2)) - ez
    dx_ey = sh.x_next(ey, after(mid, 1)) - ey
    dy_ez = sh.y_next(ez) - ez
    dy_ex = sh.y_next(ex) - ex
    hx = csub(rmul(fac.yh, dy_ez), rmul(fac.zh, hi(1, at) - ey))
    hy = csub(rmul(fac.zh, hi(0, at) - ex), rmul(xh, dx_ez))
    hz = csub(rmul(xh, dx_ey), rmul(fac.yh, dy_ex))
    bx, by, bz = (lo(c, at) for c in range(3))
    dx_bz = sh.x_next(bz, after(lo, 2)) - bz
    dy_bz = sh.y_next(bz) - bz
    hx_b = csub(rmul(fac.yh, dy_bz), rmul(fac.zb, ey - by))
    hy_b = csub(rmul(fac.zb, ex - bx), rmul(xh, dx_bz))
    curls = curl_of(fac, sh, xe, hx, hy, hz, hx_b, hy_b, before)
    out = []
    for c, e in enumerate((ex, ey, ez)):
        diagonal = 0.0 if eps is None else fac.weight * eps(c, at) * e
        out.append((curls[c][0] - diagonal, curls[c][1]))
    return out, (hy, hz)


def complex_apply(fac, sh, mid, up, below, eps, s, strips, before, shift):
    at = here(s)
    nil = (zeros(), zeros())
    after = lambda c: nil if s + 1 == strips else mid(c, here(s + 1))
    ex, ey, ez = (mid(c, at) for c in range(3))
    xh, xe = fac.x(s)
    dfx = lambda v, n: tuple(sh.x_next(a, b) - a for a, b in zip(v, n))
    dfy = lambda v: tuple(sh.y_next(a) - a for a in v)
    hx = csub(cmul(fac.yh, dfy(ez)), cmul(fac.zh, csub(up(1, at), ey)))
    hy = csub(cmul(fac.zh, csub(up(0, at), ex)), cmul(xh, dfx(ez, after(2))))
    hz = csub(cmul(xh, dfx(ey, after(1))), cmul(fac.yh, dfy(ex)))
    hx_b, hy_b = below(ex, ey)
    curls = curl_of(fac, sh, xe, hx, hy, hz, hx_b, hy_b, before)
    out = []
    for c, e in enumerate((ex, ey, ez)):
        diagonal = fac.weight * eps(c, at) + shift
        out.append(tuple(curls[c][p] - diagonal * e[p] for p in range(2)))
    return out, (hy, hz)


def plane_of(ref, q):
    return lambda c, at: ref[3 * q + c, at, :]


def eps_of(ref, first=6):
    return lambda c, at: ref[first + c, at, :]


def either(mask, yes, no):
    return lambda c, at: jnp.where(mask, yes(c, at), no(c, at))


def field_of(uxy, uz, q):
    def read(c, at):
        ref = uz.at[q] if c == 2 else uxy.at[c, q]
        return ref[0, at, :], ref[1, at, :]

    return read


def side_of(ref, q):
    return lambda c, at: tuple(part_of(ref, c)[q, p, at, :] for p in range(2))


def either_pair(mask, yes, no):
    def read(c, at):
        return tuple(jnp.where(mask, a, b) for a, b in zip(yes(c, at), no(c, at)))

    return read


def part_of(ref, c):
    return ref[c] if isinstance(ref, tuple) else ref.at[c]


def store_sends(fac, sh, field, ez_n, q, s, sc, sz):
    at = here(s)
    xh, _ = fac.x(s)
    ex, ey, ez = field
    dx_ez = tuple(sh.x_next(a, b) - a for a, b in zip(ez, ez_n))
    dy_ez = tuple(sh.y_next(a) - a for a in ez)
    part_x = cadd(cmul(fac.yh, dy_ez), cmul(fac.zh, ey))
    part_y = cadd(cmul(fac.zh, ex), cmul(xh, dx_ez))
    part_y = (-part_y[0], -part_y[1])
    for c, (down, above) in enumerate(((ex, part_x), (ey, part_y))):
        for p in range(2):
            if sc is not None:
                part_of(sc, c)[q, p, at, :] = jnp.where(fac.upper_core, down[p], above[p])
            if sz is not None:
                sz[c, q, p, at, :] = jnp.where(fac.upper_core, above[p], down[p])


def store_field(field, q, s, uxy, uz):
    for p in range(2):
        for c in range(2):
            uxy[c, q, p, here(s), :] = field[c][p]
        uz[q, p, here(s), :] = field[2][p]


def with_sends(fac, sh, q, strips, sc, sz, strips_of):
    held = []

    def store(field, s):
        if held:
            store_sends(fac, sh, held.pop(), field[2], q, s - 1, sc, sz)
        held.append(field)

    strips_of(store)
    store_sends(fac, sh, held.pop(), (zeros(), zeros()), q, strips - 1, sc, sz)


def real_strips(fac, sh, lo, mid, hi, eps, strips, store):
    before = no_strip()
    for s in range(strips):
        field, before = real_apply(fac, sh, lo, mid, hi, eps, s, strips, before)
        store(field, s)


def complex_strips(fac, sh, eps, uxy, uz, rc, rz, q, strips, shift, store):
    core = fac.upper_core
    before = no_strip()
    up = either_pair(core, side_of(rz, q), side_of(rc, q))
    dn = either_pair(core, side_of(rc, q), side_of(rz, q))
    for s in range(strips):

        def below(ex, ey):
            at = here(s)
            return csub(dn(0, at), cmul(fac.zb, ey)), cadd(dn(1, at), cmul(fac.zb, ex))

        field, before = complex_apply(
            fac, sh, field_of(uxy, uz, q), up, below, eps, s, strips, before, shift
        )
        store(field, s)


def masked(fac, field):
    return [tuple(v * fac.inside for v in pair) for pair in field]


def pack_kernel(sources, eps, out):
    out[0:6] = sources[0:6]
    out[6:9] = eps[eps.shape[0] - 3 :]


def own_kernel(strips, x, ca, za, fx, fv, uxy, uz, scx, scy, sz):
    fac, sh = Factors(fv, fx), Shifts()
    core = fac.upper_core
    for q in range(2):
        hi = either(core, plane_of(za, q), plane_of(ca, q))
        lo = either(core, plane_of(ca, q), plane_of(za, q))

        def run(store):
            def both(field, s):
                store_field(field, q, s, uxy, uz)
                store(field, s)

            real_strips(fac, sh, lo, plane_of(x, q), hi, eps_of(x), strips, both)

        with_sends(fac, sh, q, strips, (scx, scy), sz, run)


def side_kernel(strips, x, za, zb, fx, fv, uxy, uz, rz):
    fac, sh = Factors(fv, fx, CHIP), Shifts()
    core = fac.upper_core
    for q in range(2):
        hi = either(core, plane_of(zb, q), plane_of(x, q))
        lo = either(core, plane_of(x, q), plane_of(zb, q))

        def run(store):
            def both(field, s):
                field = masked(fac, field)
                store_field(field, q, s, uxy, uz)
                store(field, s)

            real_strips(fac, sh, lo, plane_of(za, q), hi, eps_of(zb), strips, both)

        with_sends(fac, sh, q, strips, rz, None, run)


def second_kernel(strips, x, u1xy, u1z, rcx, rcy, rz, fx, fv, uxy, uz, sc):
    fac, sh = Factors(fv, fx), Shifts()
    for q in range(2):

        def run(store):
            def both(field, s):
                store_field(field, q, s, uxy, uz)
                store(field, s)

            complex_strips(
                fac, sh, eps_of(x), u1xy, u1z, (rcx, rcy), rz, q, strips, SHIFT[1], both
            )

        with_sends(fac, sh, q, strips, sc, None, run)


def behind_kernel(strips, za, zb, fx, fv, rz):
    fac, sh = Factors(fv, fx, BEHIND), Shifts()
    core = fac.upper_core
    for q in range(2):
        near = plane_of(za, q)
        hi = lambda c, at: jnp.where(core, 0.0, near(c, at))
        lo = lambda c, at: jnp.where(core, near(c, at), 0.0)

        def run(store):
            masked_store = lambda field, s: store(masked(fac, field), s)
            real_strips(fac, sh, lo, plane_of(zb, q), hi, None, strips, masked_store)

        with_sends(fac, sh, q, strips, rz, None, run)


def side_second_kernel(strips, zb, rz, sz, side_xy, side_z, fx, fv, out):
    fac, sh = Factors(fv, fx, CHIP), Shifts()
    for q in range(2):

        def run(store):
            masked_store = lambda field, s: store(masked(fac, field), s)
            complex_strips(
                fac, sh, eps_of(zb), side_xy, side_z, sz, rz, q, strips, SHIFT[1], masked_store
            )

        with_sends(fac, sh, q, strips, out, None, run)


def halo_form(fac, sh, zh, s, fields, ez_n):
    ex, ey, ez = fields
    xh, _ = fac.x(s)
    part_x = cadd(rmul(fac.yh, sh.y_next(ez) - ez), rmul(zh, ey))
    part_y = csub(rmul(zh, -ex), rmul(xh, sh.x_next(ez, ez_n) - ez))
    return [
        (jnp.where(fac.upper_core, down, above[0]), jnp.where(fac.upper_core, 0.0, above[1]))
        for down, above in ((ex, part_x), (ey, part_y))
    ]


def far_kernel(strips, rz, zb, zc, fx, fv, out):
    fac, sh = Factors(fv, fx, BEHIND), Shifts()
    near_way, far_way = (fv[28], fv[29]), (fv[30], fv[31])
    for q in range(2):

        def scaled(c, at):
            return zc[6 + c, at, :] * zb[3 * q + c, at, :]

        def far(c, at):
            return zc[3 * q + c, at, :]

        for s in range(strips):
            at = here(s)
            forms = []
            for read, zh in ((scaled, fac.zh), (far, fac.zb)):
                ez_n = zeros() if s + 1 == strips else read(2, here(s + 1))
                forms.append(halo_form(fac, sh, zh, s, [read(c, at) for c in range(3)], ez_n))
            for c in range(2):
                diagonal = (fac.weight * forms[0][c][0], fac.weight * forms[0][c][1])
                change = cmul(near_way, cadd(diagonal, cmul(far_way, forms[1][c])))
                for p in range(2):
                    out[c, q, p, at, :] = rz[c, q, p, at, :] + change[p]


def third_kernel(strips, before, x, u1xy, u1z, u2xy, u2z, rc, rz, fx, fv, row):
    fac, sh = Factors(fv, fx), Shifts()
    sums = {}
    for q in range(2):

        def store(u3, s):
            u = [source_of(x, q, s), strip_of(u1xy, u1z, q, s), strip_of(u2xy, u2z, q, s), u3]
            for g, (i, j) in enumerate(GRAM):
                if j == 3:
                    add_sums(sums, g, q, dot_strip(u[i], u[j]))

        complex_strips(fac, sh, eps_of(x), u2xy, u2z, rc, rz, q, strips, SHIFT[2], store)
    row[...] = jnp.broadcast_to(before[...] + gather_sums(sums), row.shape)


def strip_of(uxy, uz, q, s):
    at = pl.ds(s * ROWS, ROWS)
    return [tuple(uxy[c, q, p, at, :] for p in range(2)) for c in range(2)] + [
        tuple(uz[q, p, at, :] for p in range(2))
    ]


def source_of(x, q, s):
    return [(x[3 * q + c, here(s), :],) for c in range(3)]


def times(a, b):
    if len(a) == 1 and len(b) == 1:
        return (a[0] * b[0],)
    if len(a) == 1:
        return a[0] * b[0], a[0] * b[1]
    if len(b) == 1:
        return a[0] * b[0], a[1] * b[0]
    return cmul(a, b)


def dot_strip(left, right):
    total = None
    for a, b in zip(left, right):
        term = times(a, b)
        total = term if total is None else tuple(x + y for x, y in zip(total, term))
    return total


def gather_sums(sums):
    lane = lax.broadcasted_iota(jnp.int32, (1, LANES), 1)
    row = jnp.zeros((1, LANES), jnp.float32)
    for (g, q, p), block in sums.items():
        folded = jnp.sum(block, axis=0, keepdims=True)
        whole = jnp.sum(folded, axis=1, keepdims=True)
        row = jnp.where(lane == 4 * g + 2 * p + q, whole, row)
    return row


def add_sums(sums, g, q, term):
    for p, block in enumerate(term):
        key = (g, q, p)
        sums[key] = block if key not in sums else sums[key] + block


def sums_kernel(strips, b, uxy, uz, row):
    sums = {}
    for q in range(2):
        for s in range(strips):
            u = [source_of(b, q, s), strip_of(uxy, uz, q, s)]
            for g, (i, j) in enumerate(GRAM):
                if j < 2:
                    add_sums(sums, g, q, dot_strip(u[i], u[j]))
    row[...] = gather_sums(sums)


def products_kernel(strips, before, b, u1xy, u1z, u2xy, u2z, row, products):
    sums = {}
    for s in range(strips):
        at = pl.ds(s * ROWS, ROWS)
        both = []
        for q in range(2):
            u = [source_of(b, q, s), strip_of(u1xy, u1z, q, s), strip_of(u2xy, u2z, q, s)]
            both.append(u)
            for g, (i, j) in enumerate(GRAM):
                if j == 2:
                    add_sums(sums, g, q, dot_strip(u[i], u[j]))
        place = 0
        for i, j in PRODUCTS:
            for part in dot_strip(both[0][i], both[1][j]):
                products[place, at, :] = part
                place += 1
    row[...] = before[...] + gather_sums(sums)


def coefficients(gram):
    def image_of(v):
        out = [None] * 4
        for i, value in enumerate(v):
            if value is None:
                continue
            out[i + 1] = value if out[i + 1] is None else cadd(out[i + 1], value)
            if SHIFT[i] != 0.0:
                moved = (SHIFT[i] * value[0], SHIFT[i] * value[1])
                out[i] = moved if out[i] is None else cadd(out[i], moved)
        return out

    def plus(a, b):
        if a is None:
            return b
        return a if b is None else cadd(a, b)

    def less(a, b):
        if b is None:
            return a
        return (-b[0], -b[1]) if a is None else csub(a, b)

    def scaled(factor, v):
        return [None if x is None else cmul(factor, x) for x in v]

    def form(left, right):
        total = None
        for i, a in enumerate(left):
            if a is None:
                continue
            inner = None
            for j, b in enumerate(right):
                if b is not None:
                    inner = plus(inner, cmul(b, gram[min(i, j), max(i, j)]))
            total = plus(total, cmul(a, inner))
        return total

    one = jnp.ones_like(gram[0, 0][0])
    residual = [(one, jnp.zeros_like(one)), None, None, None]
    image = [None, (one, jnp.zeros_like(one)), None, None]
    direction, pushed = residual, image
    rho, size = gram[0, 1], gram[1, 1]
    solution = [None] * 4
    for iteration in range(3):
        step = cdiv(rho, size)
        solution = [plus(a, b) for a, b in zip(solution, scaled(step, direction))]
        if iteration == 2:
            break
        residual = [less(a, b) for a, b in zip(residual, scaled(step, pushed))]
        image = image_of(residual[:3])
        rho_next = form(residual, image)
        ratio = cdiv(rho_next, rho)
        direction = [plus(a, b) for a, b in zip(residual, scaled(ratio, direction))]
        pushed = [plus(a, b) for a, b in zip(image, scaled(ratio, pushed))]
        size = form(pushed, pushed)
        rho = rho_next
    return solution[:3]


def gradient_kernel(strips, slabs, place, rows, products, fv, *outs):
    total = jnp.sum(rows[...], axis=0, keepdims=True)
    lane, sub = laneids(), rowids()
    spread = jnp.broadcast_to(total, (ROWS, LANES))
    gram = {}
    for g, pair in enumerate(GRAM):
        parts = []
        for p in range(2):
            mine = lane == 4 * g + 2 * p + sub
            picked = jnp.sum(jnp.where(mine, spread, 0.0), axis=1, keepdims=True)
            parts.append(jnp.broadcast_to(picked, (ROWS, LANES)))
        gram[pair] = tuple(parts)
    coefs = coefficients(gram)
    scale = fv[4] * fv[6]
    one_row = lambda v, q: jnp.broadcast_to(v[q : q + 1, :], (ROWS, LANES))
    weights = []
    for i, j in PRODUCTS:
        left = tuple(one_row(x, 0) for x in coefs[i])
        right = tuple(one_row(x, 1) for x in coefs[j])
        both = cmul(left, right)
        weights.append(both[0] * scale)
        if (i, j) != (0, 0):
            weights.append(-both[1] * scale)
    mine, shares = lax.div(place[0], slabs), len(outs)
    for k, out in enumerate(outs):
        theirs = lax.rem(mine + k, shares) * (strips // shares)
        for s in range(strips // shares):
            at = pl.ds(pl.multiple_of((theirs + s) * ROWS, ROWS), ROWS)
            value = None
            for n, weight in enumerate(weights):
                term = weight * products[n, at, :]
                value = term if value is None else value + term
            out[here(s), :] = value


def call(kernel, outs, *args, smem=0, name=None, flops=0, cost=1, scratch=()):
    specs = [pl.BlockSpec(memory_space=pltpu.SMEM if i < smem else VM) for i in range(len(args))]
    shapes = [jax.ShapeDtypeStruct(s, jnp.float32) for s in outs]
    outs_spec = [pl.BlockSpec(memory_space=VM) for _ in outs]
    return pl.pallas_call(
        kernel,
        out_shape=shapes,
        in_specs=specs,
        out_specs=outs_spec,
        scratch_shapes=[VM(s, jnp.float32) for s in scratch],
        name=name,
        cost_estimate=pl.CostEstimate(flops=flops, bytes_accessed=cost, transcendentals=0),
        compiler_params=pltpu.CompilerParams(vmem_limit_bytes=12 * 1024 * 1024),
    )(*args)


def partial(fn, *args):
    def inner(*refs):
        fn(*args, *refs)

    return inner


def body(source_fwd, source_adj, permittivity, omegas, pml_widths, design_mask):
    slabs = lax.axis_size("gz")
    shares = lax.axis_size("wl")
    rows_x, rows_y = source_fwd.shape[3], source_fwd.shape[4]
    strips = rows_x // ROWS
    core_pairs = [(i, i ^ 1) for i in range(slabs)]
    chip_pairs = []
    for i in range(1, slabs - 1, 2):
        chip_pairs += [(i, i + 1), (i + 1, i)]
    behind_pairs = [(i, i + 2) for i in range(0, slabs - 2, 2)]
    behind_pairs += [(i, i - 2) for i in range(3, slabs, 2)]
    place = lax.axis_index(("wl", "gz")).astype(jnp.int32).reshape(1)
    x = jnp.concatenate(
        [a.reshape(3, rows_x, rows_y) for a in (source_fwd, source_adj, permittivity)], axis=0
    )
    field = (2, 2, 2, rows_x, rows_y)
    plain = (2, 2, rows_x, rows_y)

    def behind(value):
        return lax.ppermute(value, "gz", behind_pairs)

    def core_swap(value):
        return lax.ppermute(value, "gz", core_pairs)

    x = lax.optimization_barrier(x)
    za = lax.ppermute(x[:6], "gz", chip_pairs)
    ca = core_swap(x)
    slab = lax.axis_index("gz")
    numbers = [omegas, pml_widths, design_mask, slab.reshape(1), (slab % 2).reshape(1)]
    small = jnp.concatenate([n.astype(jnp.float32) for n in numbers]).reshape(1, 7)
    fx, fv = call(
        partial(factor_kernel, slabs, rows_x),
        [(4, rows_x, rows_y), (FACTOR_BLOCKS, ROWS, LANES)],
        small,
        name="factors",
    )
    ca, fx, fv, place = lax.optimization_barrier((ca, fx, fv, place))
    (pack,) = call(pack_kernel, [(9, rows_x, rows_y)], x, ca, name="pack")
    zb = behind(pack)
    (relay,) = call(pack_kernel, [(9, rows_x, rows_y)], za, x, name="pack_relay")
    zc = behind(relay)
    u1xy, u1z, scx, scy, sz = call(
        partial(own_kernel, strips),
        [field, plain, plain, plain, field],
        x,
        ca,
        za,
        fx,
        fv,
        name="apply_own",
    )
    rcx, rcy = core_swap(scx), core_swap(scy)
    side_xy, side_z, rz = call(
        partial(side_kernel, strips), [field, plain, field], x, za, zb, fx, fv, name="apply_side"
    )
    (row,) = call(partial(sums_kernel, strips), [(1, LANES)], x, u1xy, u1z, name="sums")
    u2xy, u2z, sc = call(
        partial(second_kernel, strips),
        [field, plain, field],
        x,
        u1xy,
        u1z,
        rcx,
        rcy,
        rz,
        fx,
        fv,
        name="apply_second",
    )
    rc = core_swap(sc)
    row, products = call(
        partial(products_kernel, strips),
        [(1, LANES), (2 * len(PRODUCTS) - 1, rows_x, rows_y)],
        row,
        x,
        u1xy,
        u1z,
        u2xy,
        u2z,
        name="products",
    )
    sz, row, products = lax.optimization_barrier((sz, row, products))
    (rz,) = call(partial(behind_kernel, strips), [field], za, zb, fx, fv, name="apply_behind")
    (rz,) = call(
        partial(side_second_kernel, strips),
        [field],
        zb,
        rz,
        sz,
        side_xy,
        side_z,
        fx,
        fv,
        name="apply_side_second",
    )
    (rz,) = call(
        partial(far_kernel, strips),
        [field],
        rz,
        zb,
        zc,
        fx,
        fv,
        name="add_far",
        flops=1 << 36,
        cost=1 << 27,
    )
    (rows,) = call(
        partial(third_kernel, strips),
        [(slabs, LANES)],
        row,
        x,
        u1xy,
        u1z,
        u2xy,
        u2z,
        rc,
        rz,
        fx,
        fv,
        name="apply_third",
    )
    rows = lax.all_to_all(rows, "gz", 0, 0)
    parts = call(
        partial(gradient_kernel, strips, slabs),
        [(rows_x // shares, rows_y)] * shares,
        place,
        rows,
        products,
        fv,
        smem=1,
        name="gradient",
    )
    total = parts[0]
    for k in range(1, shares):
        total = total + lax.ppermute(parts[k], "wl", [(i, (i + k) % shares) for i in range(shares)])
    return total[None]


def solution(mesh):
    return jax.shard_map(
        body,
        mesh=mesh,
        in_specs=(
            P("wl", None, "gz", None, None),
            P("wl", None, "gz", None, None),
            P(None, "gz", None, None),
            P("wl"),
            P(),
            P("gz"),
        ),
        out_specs=P("gz", "wl", None),
        check_vma=False,
    )
```

```python
import jax
import jax.numpy as jnp
from jax import lax
from jax.experimental import pallas as pl
from jax.experimental.pallas import tpu as pltpu
from jax.sharding import PartitionSpec as P

SIGMA_MAX = 1.0
SHIFT = (0.0, 6.0, 12.0)
ROWS = 8
WIDEST = 4
LANES = 128
GRAM = [(0, 0), (0, 1), (1, 1), (0, 2), (1, 2), (2, 2), (0, 3), (1, 3), (2, 3), (3, 3)]
PRODUCTS = [(i, j) for i in range(3) for j in range(3)]
VM = pltpu.VMEM


def cmul(a, b):
    if a is None:
        return b
    return a[0] * b[0] - a[1] * b[1], a[0] * b[1] + a[1] * b[0]


def cadd(a, b):
    return a[0] + b[0], a[1] + b[1]


def csub(a, b):
    return minus(a[0], b[0]), minus(a[1], b[1])


def minus(a, b):
    if isinstance(b, float):
        return a
    return -b if isinstance(a, float) else a - b


def cdiv(upper, lower):
    den = lower[0] * lower[0] + lower[1] * lower[1]
    return (
        (upper[0] * lower[0] + upper[1] * lower[1]) / den,
        (upper[1] * lower[0] - upper[0] * lower[1]) / den,
    )


def rowids():
    return lax.broadcasted_iota(jnp.int32, (ROWS, LANES), 0)


def laneids():
    return lax.broadcasted_iota(jnp.int32, (ROWS, LANES), 1)


class Shifts:
    def __init__(self):
        self.first_row = rowids() == 0
        self.last_row = rowids() == ROWS - 1
        self.first_lane = laneids() == 0
        self.last_lane = laneids() == LANES - 1

    def x_next(self, cur, nxt):
        return pltpu.roll(jnp.where(self.first_row, nxt, cur), ROWS - 1, 0)

    def x_prev(self, cur, prv):
        return pltpu.roll(jnp.where(self.last_row, prv, cur), 1, 0)

    def y_next(self, cur):
        return jnp.where(self.last_lane, 0.0, pltpu.roll(cur, LANES - 1, 1))

    def y_prev(self, cur):
        return jnp.where(self.first_lane, 0.0, pltpu.roll(cur, 1, 1))


def profile(positions, length, width, angular):
    depth = jnp.clip(jnp.maximum(width - positions, positions - (length - 1 - width)), 0.0, width)
    part = depth / width
    ratios = SIGMA_MAX * (part * part * part) / angular
    denominator = 1.0 + ratios * ratios
    return 1.0 / denominator, -ratios / denominator


def factor_kernel(total_planes, rows_x, small, fx, fv):
    angular, wx, wy, wz, mask, slab, upper = (
        jnp.broadcast_to(small[:, n : n + 1], (ROWS, LANES)) for n in range(7)
    )
    for s in range(rows_x // ROWS):
        pos = (rowids() + s * ROWS).astype(jnp.float32)
        at = pl.ds(s * ROWS, ROWS)
        fx[0, at, :], fx[1, at, :] = profile(pos + 0.5, rows_x, wx, angular)
        fx[2, at, :], fx[3, at, :] = profile(pos, rows_x, wx, angular)
    pos = laneids().astype(jnp.float32)
    fv[0], fv[1] = profile(pos + 0.5, LANES, wy, angular)
    fv[2], fv[3] = profile(pos, LANES, wy, angular)
    fv[4] = angular * angular
    fv[5] = upper
    fv[6] = mask
    side = 1.0 - 2.0 * upper
    for n, plane in enumerate((slab, slab - side, slab - 2.0 * side)):
        low = 7 + 7 * n
        fv[low], fv[low + 1] = profile(plane + 0.5, total_planes, wz, angular)
        fv[low + 2], fv[low + 3] = profile(plane, total_planes, wz, angular)
        below_re, below_im = profile(plane - 0.5, total_planes, wz, angular)
        above_floor = plane > 0.0
        fv[low + 4] = jnp.where(above_floor, below_re, 0.0)
        fv[low + 5] = jnp.where(above_floor, below_im, 0.0)
        inside = (plane >= 0.0) & (plane < total_planes)
        fv[low + 6] = jnp.where(inside, 1.0, 0.0)
    for at, low in ((28, 14), (30, 21)):
        way = cmul((fv[low], fv[low + 1]), (fv[low + 2], fv[low + 3]))
        fv[at], fv[at + 1] = way[0] * fv[low + 6], way[1] * fv[low + 6]


OWN, CHIP, BEHIND = 0, 1, 2
FACTOR_BLOCKS = 32


class Factors:
    def __init__(self, fv, fx, which=OWN):
        low = 7 + 7 * which
        self.yh = (fv[0], fv[1])
        self.ye = (fv[2], fv[3])
        self.weight = fv[4]
        self.upper_core = fv[5] > 0.5
        self.zh = (fv[low], fv[low + 1])
        self.ze = (fv[low + 2], fv[low + 3])
        self.zb = (fv[low + 4], fv[low + 5])
        self.inside = fv[low + 6]
        self.fx = fx

    def x(self, s):
        if s * ROWS >= WIDEST and s * ROWS + ROWS - 0.5 <= self.fx.shape[1] - 1 - WIDEST:
            return None, None
        at = pl.ds(s * ROWS, ROWS)
        return (self.fx[0, at, :], self.fx[1, at, :]), (self.fx[2, at, :], self.fx[3, at, :])


def zeros():
    return jnp.zeros((ROWS, LANES), jnp.float32)


def no_strip():
    nil = (zeros(), zeros())
    return nil, nil


def rmul(factor, real):
    if factor is None:
        return real, 0.0
    return factor[0] * real, factor[1] * real


def here(s):
    return pl.ds(s * ROWS, ROWS)


def curl_of(fac, sh, xe, hx, hy, hz, hx_b, hy_b, before):
    hy_p, hz_p = before
    dby = lambda h: tuple(p - sh.y_prev(p) for p in h)
    dbx = lambda h, q: tuple(p - sh.x_prev(p, r) for p, r in zip(h, q))
    cx = csub(cmul(fac.ye, dby(hz)), cmul(fac.ze, csub(hy, hy_b)))
    cy = csub(cmul(fac.ze, csub(hx, hx_b)), cmul(xe, dbx(hz, hz_p)))
    cz = csub(cmul(xe, dbx(hy, hy_p)), cmul(fac.ye, dby(hx)))
    return cx, cy, cz


def real_apply(fac, sh, lo, mid, hi, eps, s, strips, before):
    at = here(s)
    after = lambda of, c: zeros() if s + 1 == strips else of(c, here(s + 1))
    ex, ey, ez = (mid(c, at) for c in range(3))
    xh, xe = fac.x(s)
    dx_ez = sh.x_next(ez, after(mid, 2)) - ez
    dx_ey = sh.x_next(ey, after(mid, 1)) - ey
    dy_ez = sh.y_next(ez) - ez
    dy_ex = sh.y_next(ex) - ex
    hx = csub(rmul(fac.yh, dy_ez), rmul(fac.zh, hi(1, at) - ey))
    hy = csub(rmul(fac.zh, hi(0, at) - ex), rmul(xh, dx_ez))
    hz = csub(rmul(xh, dx_ey), rmul(fac.yh, dy_ex))
    bx, by, bz = (lo(c, at) for c in range(3))
    dx_bz = sh.x_next(bz, after(lo, 2)) - bz
    dy_bz = sh.y_next(bz) - bz
    hx_b = csub(rmul(fac.yh, dy_bz), rmul(fac.zb, ey - by))
    hy_b = csub(rmul(fac.zb, ex - bx), rmul(xh, dx_bz))
    curls = curl_of(fac, sh, xe, hx, hy, hz, hx_b, hy_b, before)
    out = []
    for c, e in enumerate((ex, ey, ez)):
        diagonal = 0.0 if eps is None else fac.weight * eps(c, at) * e
        out.append((curls[c][0] - diagonal, curls[c][1]))
    return out, (hy, hz)


def complex_apply(fac, sh, mid, up, below, eps, s, strips, before, shift):
    at = here(s)
    nil = (zeros(), zeros())
    after = lambda c: nil if s + 1 == strips else mid(c, here(s + 1))
    ex, ey, ez = (mid(c, at) for c in range(3))
    xh, xe = fac.x(s)
    dfx = lambda v, n: tuple(sh.x_next(a, b) - a for a, b in zip(v, n))
    dfy = lambda v: tuple(sh.y_next(a) - a for a in v)
    hx = csub(cmul(fac.yh, dfy(ez)), cmul(fac.zh, csub(up(1, at), ey)))
    hy = csub(cmul(fac.zh, csub(up(0, at), ex)), cmul(xh, dfx(ez, after(2))))
    hz = csub(cmul(xh, dfx(ey, after(1))), cmul(fac.yh, dfy(ex)))
    hx_b, hy_b = below(ex, ey)
    curls = curl_of(fac, sh, xe, hx, hy, hz, hx_b, hy_b, before)
    out = []
    for c, e in enumerate((ex, ey, ez)):
        diagonal = fac.weight * eps(c, at) + shift
        out.append(tuple(curls[c][p] - diagonal * e[p] for p in range(2)))
    return out, (hy, hz)


def plane_of(ref, q):
    return lambda c, at: ref[3 * q + c, at, :]


def eps_of(ref, first=6):
    return lambda c, at: ref[first + c, at, :]


def either(mask, yes, no):
    return lambda c, at: jnp.where(mask, yes(c, at), no(c, at))


def field_of(uxy, uz, q):
    def read(c, at):
        ref = uz.at[q] if c == 2 else uxy.at[c, q]
        return ref[0, at, :], ref[1, at, :]

    return read


def side_of(ref, q):
    return lambda c, at: tuple(part_of(ref, c)[q, p, at, :] for p in range(2))


def either_pair(mask, yes, no):
    def read(c, at):
        return tuple(jnp.where(mask, a, b) for a, b in zip(yes(c, at), no(c, at)))

    return read


def part_of(ref, c):
    return ref[c] if isinstance(ref, tuple) else ref.at[c]


def store_sends(fac, sh, field, ez_n, q, s, sc, sz):
    at = here(s)
    xh, _ = fac.x(s)
    ex, ey, ez = field
    dx_ez = tuple(sh.x_next(a, b) - a for a, b in zip(ez, ez_n))
    dy_ez = tuple(sh.y_next(a) - a for a in ez)
    part_x = cadd(cmul(fac.yh, dy_ez), cmul(fac.zh, ey))
    part_y = cadd(cmul(fac.zh, ex), cmul(xh, dx_ez))
    part_y = (-part_y[0], -part_y[1])
    for c, (down, above) in enumerate(((ex, part_x), (ey, part_y))):
        for p in range(2):
            if sc is not None:
                part_of(sc, c)[q, p, at, :] = jnp.where(fac.upper_core, down[p], above[p])
            if sz is not None:
                sz[c, q, p, at, :] = jnp.where(fac.upper_core, above[p], down[p])


def store_field(field, q, s, uxy, uz):
    for p in range(2):
        for c in range(2):
            uxy[c, q, p, here(s), :] = field[c][p]
        uz[q, p, here(s), :] = field[2][p]


def with_sends(fac, sh, q, strips, sc, sz, strips_of):
    held = []

    def store(field, s):
        if held:
            store_sends(fac, sh, held.pop(), field[2], q, s - 1, sc, sz)
        held.append(field)

    strips_of(store)
    store_sends(fac, sh, held.pop(), (zeros(), zeros()), q, strips - 1, sc, sz)


def real_strips(fac, sh, lo, mid, hi, eps, strips, store):
    before = no_strip()
    for s in range(strips):
        field, before = real_apply(fac, sh, lo, mid, hi, eps, s, strips, before)
        store(field, s)


def complex_strips(fac, sh, eps, uxy, uz, rc, rz, q, strips, shift, store):
    core = fac.upper_core
    before = no_strip()
    up = either_pair(core, side_of(rz, q), side_of(rc, q))
    dn = either_pair(core, side_of(rc, q), side_of(rz, q))
    for s in range(strips):

        def below(ex, ey):
            at = here(s)
            return csub(dn(0, at), cmul(fac.zb, ey)), cadd(dn(1, at), cmul(fac.zb, ex))

        field, before = complex_apply(
            fac, sh, field_of(uxy, uz, q), up, below, eps, s, strips, before, shift
        )
        store(field, s)


def masked(fac, field):
    return [tuple(v * fac.inside for v in pair) for pair in field]


def pack_kernel(sources, eps, out):
    out[0:6] = sources[0:6]
    out[6:9] = eps[eps.shape[0] - 3 :]


def own_kernel(strips, x, ca, za, fx, fv, uxy, uz, scx, scy, sz):
    fac, sh = Factors(fv, fx), Shifts()
    core = fac.upper_core
    for q in range(2):
        hi = either(core, plane_of(za, q), plane_of(ca, q))
        lo = either(core, plane_of(ca, q), plane_of(za, q))

        def run(store):
            def both(field, s):
                store_field(field, q, s, uxy, uz)
                store(field, s)

            real_strips(fac, sh, lo, plane_of(x, q), hi, eps_of(x), strips, both)

        with_sends(fac, sh, q, strips, (scx, scy), sz, run)


def side_kernel(strips, x, za, zb, fx, fv, uxy, uz, rz):
    fac, sh = Factors(fv, fx, CHIP), Shifts()
    core = fac.upper_core
    for q in range(2):
        hi = either(core, plane_of(zb, q), plane_of(x, q))
        lo = either(core, plane_of(x, q), plane_of(zb, q))

        def run(store):
            def both(field, s):
                field = masked(fac, field)
                store_field(field, q, s, uxy, uz)
                store(field, s)

            real_strips(fac, sh, lo, plane_of(za, q), hi, eps_of(zb), strips, both)

        with_sends(fac, sh, q, strips, rz, None, run)


def second_kernel(strips, x, u1xy, u1z, rcx, rcy, rz, fx, fv, uxy, uz, sc):
    fac, sh = Factors(fv, fx), Shifts()
    for q in range(2):

        def run(store):
            def both(field, s):
                store_field(field, q, s, uxy, uz)
                store(field, s)

            complex_strips(
                fac, sh, eps_of(x), u1xy, u1z, (rcx, rcy), rz, q, strips, SHIFT[1], both
            )

        with_sends(fac, sh, q, strips, sc, None, run)


def behind_kernel(strips, za, zb, fx, fv, rz):
    fac, sh = Factors(fv, fx, BEHIND), Shifts()
    core = fac.upper_core
    for q in range(2):
        near = plane_of(za, q)
        hi = lambda c, at: jnp.where(core, 0.0, near(c, at))
        lo = lambda c, at: jnp.where(core, near(c, at), 0.0)

        def run(store):
            masked_store = lambda field, s: store(masked(fac, field), s)
            real_strips(fac, sh, lo, plane_of(zb, q), hi, None, strips, masked_store)

        with_sends(fac, sh, q, strips, rz, None, run)


def side_second_kernel(strips, zb, rz, sz, side_xy, side_z, fx, fv, out):
    fac, sh = Factors(fv, fx, CHIP), Shifts()
    for q in range(2):

        def run(store):
            masked_store = lambda field, s: store(masked(fac, field), s)
            complex_strips(
                fac, sh, eps_of(zb), side_xy, side_z, sz, rz, q, strips, SHIFT[1], masked_store
            )

        with_sends(fac, sh, q, strips, out, None, run)


def halo_form(fac, sh, zh, s, fields, ez_n):
    ex, ey, ez = fields
    xh, _ = fac.x(s)
    part_x = cadd(rmul(fac.yh, sh.y_next(ez) - ez), rmul(zh, ey))
    part_y = csub(rmul(zh, -ex), rmul(xh, sh.x_next(ez, ez_n) - ez))
    return [
        (jnp.where(fac.upper_core, down, above[0]), jnp.where(fac.upper_core, 0.0, above[1]))
        for down, above in ((ex, part_x), (ey, part_y))
    ]


def far_kernel(strips, rz, zb, zc, fx, fv, out):
    fac, sh = Factors(fv, fx, BEHIND), Shifts()
    near_way, far_way = (fv[28], fv[29]), (fv[30], fv[31])
    for q in range(2):

        def scaled(c, at):
            return zc[6 + c, at, :] * zb[3 * q + c, at, :]

        def far(c, at):
            return zc[3 * q + c, at, :]

        for s in range(strips):
            at = here(s)
            forms = []
            for read, zh in ((scaled, fac.zh), (far, fac.zb)):
                ez_n = zeros() if s + 1 == strips else read(2, here(s + 1))
                forms.append(halo_form(fac, sh, zh, s, [read(c, at) for c in range(3)], ez_n))
            for c in range(2):
                diagonal = (fac.weight * forms[0][c][0], fac.weight * forms[0][c][1])
                change = cmul(near_way, cadd(diagonal, cmul(far_way, forms[1][c])))
                for p in range(2):
                    out[c, q, p, at, :] = rz[c, q, p, at, :] + change[p]


def third_kernel(strips, before, x, u1xy, u1z, u2xy, u2z, rc, rz, fx, fv, row):
    fac, sh = Factors(fv, fx), Shifts()
    sums = {}
    for q in range(2):

        def store(u3, s):
            u = [source_of(x, q, s), strip_of(u1xy, u1z, q, s), strip_of(u2xy, u2z, q, s), u3]
            for g, (i, j) in enumerate(GRAM):
                if j == 3:
                    add_sums(sums, g, q, dot_strip(u[i], u[j]))

        complex_strips(fac, sh, eps_of(x), u2xy, u2z, rc, rz, q, strips, SHIFT[2], store)
    row[...] = jnp.broadcast_to(before[...] + gather_sums(sums), row.shape)


def strip_of(uxy, uz, q, s):
    at = pl.ds(s * ROWS, ROWS)
    return [tuple(uxy[c, q, p, at, :] for p in range(2)) for c in range(2)] + [
        tuple(uz[q, p, at, :] for p in range(2))
    ]


def source_of(x, q, s):
    return [(x[3 * q + c, here(s), :],) for c in range(3)]


def times(a, b):
    if len(a) == 1 and len(b) == 1:
        return (a[0] * b[0],)
    if len(a) == 1:
        return a[0] * b[0], a[0] * b[1]
    if len(b) == 1:
        return a[0] * b[0], a[1] * b[0]
    return cmul(a, b)


def dot_strip(left, right):
    total = None
    for a, b in zip(left, right):
        term = times(a, b)
        total = term if total is None else tuple(x + y for x, y in zip(total, term))
    return total


def gather_sums(sums):
    lane = lax.broadcasted_iota(jnp.int32, (1, LANES), 1)
    row = jnp.zeros((1, LANES), jnp.float32)
    for (g, q, p), block in sums.items():
        folded = jnp.sum(block, axis=0, keepdims=True)
        whole = jnp.sum(folded, axis=1, keepdims=True)
        row = jnp.where(lane == 4 * g + 2 * p + q, whole, row)
    return row


def add_sums(sums, g, q, term):
    for p, block in enumerate(term):
        key = (g, q, p)
        sums[key] = block if key not in sums else sums[key] + block


def sums_kernel(strips, b, uxy, uz, row):
    sums = {}
    for q in range(2):
        for s in range(strips):
            u = [source_of(b, q, s), strip_of(uxy, uz, q, s)]
            for g, (i, j) in enumerate(GRAM):
                if j < 2:
                    add_sums(sums, g, q, dot_strip(u[i], u[j]))
    row[...] = gather_sums(sums)


def products_kernel(strips, before, b, u1xy, u1z, u2xy, u2z, row, products):
    sums = {}
    for s in range(strips):
        at = pl.ds(s * ROWS, ROWS)
        both = []
        for q in range(2):
            u = [source_of(b, q, s), strip_of(u1xy, u1z, q, s), strip_of(u2xy, u2z, q, s)]
            both.append(u)
            for g, (i, j) in enumerate(GRAM):
                if j == 2:
                    add_sums(sums, g, q, dot_strip(u[i], u[j]))
        place = 0
        for i, j in PRODUCTS:
            for part in dot_strip(both[0][i], both[1][j]):
                products[place, at, :] = part
                place += 1
    row[...] = before[...] + gather_sums(sums)


def coefficients(gram):
    def image_of(v):
        out = [None] * 4
        for i, value in enumerate(v):
            if value is None:
                continue
            out[i + 1] = value if out[i + 1] is None else cadd(out[i + 1], value)
            if SHIFT[i] != 0.0:
                moved = (SHIFT[i] * value[0], SHIFT[i] * value[1])
                out[i] = moved if out[i] is None else cadd(out[i], moved)
        return out

    def plus(a, b):
        if a is None:
            return b
        return a if b is None else cadd(a, b)

    def less(a, b):
        if b is None:
            return a
        return (-b[0], -b[1]) if a is None else csub(a, b)

    def scaled(factor, v):
        return [None if x is None else cmul(factor, x) for x in v]

    def form(left, right):
        total = None
        for i, a in enumerate(left):
            if a is None:
                continue
            inner = None
            for j, b in enumerate(right):
                if b is not None:
                    inner = plus(inner, cmul(b, gram[min(i, j), max(i, j)]))
            total = plus(total, cmul(a, inner))
        return total

    one = jnp.ones_like(gram[0, 0][0])
    residual = [(one, jnp.zeros_like(one)), None, None, None]
    image = [None, (one, jnp.zeros_like(one)), None, None]
    direction, pushed = residual, image
    rho, size = gram[0, 1], gram[1, 1]
    solution = [None] * 4
    for iteration in range(3):
        step = cdiv(rho, size)
        solution = [plus(a, b) for a, b in zip(solution, scaled(step, direction))]
        if iteration == 2:
            break
        residual = [less(a, b) for a, b in zip(residual, scaled(step, pushed))]
        image = image_of(residual[:3])
        rho_next = form(residual, image)
        ratio = cdiv(rho_next, rho)
        direction = [plus(a, b) for a, b in zip(residual, scaled(ratio, direction))]
        pushed = [plus(a, b) for a, b in zip(image, scaled(ratio, pushed))]
        size = form(pushed, pushed)
        rho = rho_next
    return solution[:3]


def gradient_kernel(strips, slabs, place, rows, products, fv, *outs):
    total = jnp.sum(rows[...], axis=0, keepdims=True)
    lane, sub = laneids(), rowids()
    spread = jnp.broadcast_to(total, (ROWS, LANES))
    gram = {}
    for g, pair in enumerate(GRAM):
        parts = []
        for p in range(2):
            mine = lane == 4 * g + 2 * p + sub
            picked = jnp.sum(jnp.where(mine, spread, 0.0), axis=1, keepdims=True)
            parts.append(jnp.broadcast_to(picked, (ROWS, LANES)))
        gram[pair] = tuple(parts)
    coefs = coefficients(gram)
    scale = fv[4] * fv[6]
    one_row = lambda v, q: jnp.broadcast_to(v[q : q + 1, :], (ROWS, LANES))
    weights = []
    for i, j in PRODUCTS:
        left = tuple(one_row(x, 0) for x in coefs[i])
        right = tuple(one_row(x, 1) for x in coefs[j])
        both = cmul(left, right)
        weights.append(both[0] * scale)
        if (i, j) != (0, 0):
            weights.append(-both[1] * scale)
    mine, shares = lax.div(place[0], slabs), len(outs)
    for k, out in enumerate(outs):
        theirs = lax.rem(mine + k, shares) * (strips // shares)
        for s in range(strips // shares):
            at = pl.ds(pl.multiple_of((theirs + s) * ROWS, ROWS), ROWS)
            value = None
            for n, weight in enumerate(weights):
                term = weight * products[n, at, :]
                value = term if value is None else value + term
            out[here(s), :] = value


def call(kernel, outs, *args, smem=0, name=None, flops=0, cost=1, scratch=()):
    specs = [pl.BlockSpec(memory_space=pltpu.SMEM if i < smem else VM) for i in range(len(args))]
    shapes = [jax.ShapeDtypeStruct(s, jnp.float32) for s in outs]
    outs_spec = [pl.BlockSpec(memory_space=VM) for _ in outs]
    return pl.pallas_call(
        kernel,
        out_shape=shapes,
        in_specs=specs,
        out_specs=outs_spec,
        scratch_shapes=[VM(s, jnp.float32) for s in scratch],
        name=name,
        cost_estimate=pl.CostEstimate(flops=flops, bytes_accessed=cost, transcendentals=0),
        compiler_params=pltpu.CompilerParams(vmem_limit_bytes=12 * 1024 * 1024),
    )(*args)


def partial(fn, *args):
    def inner(*refs):
        fn(*args, *refs)

    return inner


def body(source_fwd, source_adj, permittivity, omegas, pml_widths, design_mask):
    slabs = lax.axis_size("gz")
    shares = lax.axis_size("wl")
    rows_x, rows_y = source_fwd.shape[3], source_fwd.shape[4]
    strips = rows_x // ROWS
    core_pairs = [(i, i ^ 1) for i in range(slabs)]
    chip_pairs = []
    for i in range(1, slabs - 1, 2):
        chip_pairs += [(i, i + 1), (i + 1, i)]
    behind_pairs = [(i, i + 2) for i in range(0, slabs - 2, 2)]
    behind_pairs += [(i, i - 2) for i in range(3, slabs, 2)]
    place = lax.axis_index(("wl", "gz")).astype(jnp.int32).reshape(1)
    x = jnp.concatenate(
        [a.reshape(3, rows_x, rows_y) for a in (source_fwd, source_adj, permittivity)], axis=0
    )
    field = (2, 2, 2, rows_x, rows_y)
    plain = (2, 2, rows_x, rows_y)

    def behind(value):
        return lax.ppermute(value, "gz", behind_pairs)

    def core_swap(value):
        return lax.ppermute(value, "gz", core_pairs)

    x = lax.optimization_barrier(x)
    za = lax.ppermute(x[:6], "gz", chip_pairs)
    ca = core_swap(x)
    slab = lax.axis_index("gz")
    numbers = [omegas, pml_widths, design_mask, slab.reshape(1), (slab % 2).reshape(1)]
    small = jnp.concatenate([n.astype(jnp.float32) for n in numbers]).reshape(1, 7)
    fx, fv = call(
        partial(factor_kernel, slabs, rows_x),
        [(4, rows_x, rows_y), (FACTOR_BLOCKS, ROWS, LANES)],
        small,
        name="factors",
    )
    ca, fx, fv, place = lax.optimization_barrier((ca, fx, fv, place))
    (pack,) = call(pack_kernel, [(9, rows_x, rows_y)], x, ca, name="pack")
    zb = behind(pack)
    (relay,) = call(pack_kernel, [(9, rows_x, rows_y)], za, x, name="pack_relay")
    zc = behind(relay)
    u1xy, u1z, scx, scy, sz = call(
        partial(own_kernel, strips),
        [field, plain, plain, plain, field],
        x,
        ca,
        za,
        fx,
        fv,
        name="apply_own",
    )
    rcx, rcy = core_swap(scx), core_swap(scy)
    side_xy, side_z, rz = call(
        partial(side_kernel, strips), [field, plain, field], x, za, zb, fx, fv, name="apply_side"
    )
    (row,) = call(partial(sums_kernel, strips), [(1, LANES)], x, u1xy, u1z, name="sums")
    u2xy, u2z, sc = call(
        partial(second_kernel, strips),
        [field, plain, field],
        x,
        u1xy,
        u1z,
        rcx,
        rcy,
        rz,
        fx,
        fv,
        name="apply_second",
    )
    rc = core_swap(sc)
    row, products = call(
        partial(products_kernel, strips),
        [(1, LANES), (2 * len(PRODUCTS) - 1, rows_x, rows_y)],
        row,
        x,
        u1xy,
        u1z,
        u2xy,
        u2z,
        name="products",
    )
    sz, row, products = lax.optimization_barrier((sz, row, products))
    (rz,) = call(partial(behind_kernel, strips), [field], za, zb, fx, fv, name="apply_behind")
    (rz,) = call(
        partial(side_second_kernel, strips),
        [field],
        zb,
        rz,
        sz,
        side_xy,
        side_z,
        fx,
        fv,
        name="apply_side_second",
    )
    (rz,) = call(
        partial(far_kernel, strips),
        [field],
        rz,
        zb,
        zc,
        fx,
        fv,
        name="add_far",
        flops=1 << 36,
        cost=1 << 27,
    )
    (rows,) = call(
        partial(third_kernel, strips),
        [(slabs, LANES)],
        row,
        x,
        u1xy,
        u1z,
        u2xy,
        u2z,
        rc,
        rz,
        fx,
        fv,
        name="apply_third",
    )
    rows = lax.all_to_all(rows, "gz", 0, 0)
    parts = call(
        partial(gradient_kernel, strips, slabs),
        [(rows_x // shares, rows_y)] * shares,
        place,
        rows,
        products,
        fv,
        smem=1,
        name="gradient",
    )
    total = parts[0]
    for k in sorted(range(1, shares), key=lambda k: (-min(k, shares - k), k)):
        total = total + lax.ppermute(parts[k], "wl", [(i, (i + k) % shares) for i in range(shares)])
    return total[None]


def solution(mesh):
    return jax.shard_map(
        body,
        mesh=mesh,
        in_specs=(
            P("wl", None, "gz", None, None),
            P("wl", None, "gz", None, None),
            P(None, "gz", None, None),
            P("wl"),
            P(),
            P("gz"),
        ),
        out_specs=P("gz", "wl", None),
        check_vma=False,
    )
```
